256 devices in a mesh: dp: 32 (over x_hi, z, core), tensor: 8 (over y, x_lo).
Axes of the slice: x: 4 (x_hi: 2, x_lo: 2; x = x_hi * 2 + x_lo), y: 4, z: 8, core: 2. Of those that a mesh axis runs over, the one named last changes fastest.
Arguments:
- activations: bfloat16 [16384, 6144], P('dp', 'tensor'), may hold values from -12 to 12
- out_grads: bfloat16 [16384, 3072], P('dp'), may hold values from -6 to 6
- a_basis: bfloat16 [6144, 768], P('tensor'), may hold values from -0.21875 to 0.21875
- a_values: float32 [6144], P('tensor'), may hold values from 0.3 to 3
- g_basis: bfloat16 [3072, 3072], P(None, 'dp'), may hold values from -0.109375 to 0.109375
- g_values: float32 [3072], P('dp'), may hold values from 0.3 to 3
- owners: int32 [2, 32], replicated, may hold values from 0 to 31, each once within a row
- a_factors: float32 [768, 6144], P('dp', 'tensor'), may hold values from -3 to 3
- g_factors: float32 [3072, 3072], P('dp', 'tensor'), may hold values from -3 to 3
Outputs:
- update: float32 [3072, 6144], P('dp', 'tensor')
- new_a_factors: float32 [768, 6144], P('dp', 'tensor')
- new_g_factors: float32 [3072, 3072], P('dp', 'tensor')
The draws below stay inside these ranges and needn't reach their ends.
Inputs may be any that keep to these rules, and one draw needn't show every extreme that they name: Each row of owners names every worker exactly once.
All inputs are finite; a program needn't handle non-finite values.
Results may differ from the reference program's by a relative error of at most 0.03.
Values may be sent and summed in bfloat16 or wider, within the bound.
A program may use at most 128 MiB of HBM per device.

```python
import math
import jax
import jax.numpy as jnp
from jax import lax

FEAT = 6144
OUT_WIN = 3072
TOK_DEV = 512
FEAT_SHARD = 768
TOKENS = 16384
N_DP = 32
N_TENSOR = 8


def draw_activations(key, part):
    key = jax.random.fold_in(key, 11)
    replica_pos = (jnp.arange(TOKENS, dtype=jnp.int32) // TOK_DEV).astype(jnp.float32) / max(N_DP - 1, 1)
    base = jnp.clip(jax.random.normal(key, (TOKENS, FEAT), jnp.float32), -4.0, 4.0)
    row_scale = 1.0 + 2.0 * replica_pos
    return (base * row_scale[:, None]).astype(jnp.bfloat16)


def draw_g_values(key, part):
    key = jax.random.fold_in(key, 23)
    place = jnp.arange(OUT_WIN, dtype=jnp.float32) / OUT_WIN
    ramp = 0.8
    rough = jax.random.uniform(key, (OUT_WIN,), jnp.float32, 0.0, 1.0 - ramp)
    return (0.3 * jnp.exp(2.3025851 * (ramp * place + rough))).astype(jnp.float32)


def level_of(stream_key, shape, shards, least, largest):
    def one(axis_at, blocks):
        draws = jax.random.uniform(jax.random.fold_in(jax.random.fold_in(stream_key, 6), axis_at), (blocks,), jnp.float32, least / len(shards), largest / len(shards))
        return jnp.repeat(jnp.exp(draws), shape[axis_at] // blocks).reshape((-1,) + (1,) * (len(shape) - axis_at - 1))

    level = one(*shards[0])
    for cut in shards[1:]:
        level = level * one(*cut)
    return level


def centred(key, dims, scale, limit, cuts=(), kind=jnp.bfloat16):
    result = jax.random.normal(key, dims, jnp.float32) * scale
    if len(cuts) > 0:
        result = level_of(key, dims, cuts, -0.22, 0.18) * result
    return jnp.clip(result, min=-limit, max=limit).astype(kind)


def setup_inputs(seed: int = 0) -> dict:
    arg_keys = jax.random.split(jax.random.key(seed), 10)
    activations = draw_activations(jax.random.fold_in(arg_keys[9], 71), 0)
    out_grads = centred(arg_keys[1], (TOKENS, OUT_WIN), 1.0, 6.0, ((0, 32),))
    a_basis = centred(arg_keys[2], (FEAT, FEAT_SHARD), (FEAT // N_TENSOR) ** -0.5, 0.21875, ((0, 8),))
    a_values = jnp.clip(jnp.exp(math.log(3.0) - 2.3025851 * jax.random.uniform(arg_keys[3], (FEAT,), jnp.float32) ** level_of(arg_keys[3], (FEAT,), ((0, 8),), -0.2, 0.2)), 0.3, 3.0)
    g_basis = centred(arg_keys[4], (OUT_WIN, OUT_WIN), OUT_WIN ** -0.5, 0.109375, ((1, 32),))
    g_values = draw_g_values(jax.random.fold_in(arg_keys[9], 71), 0)
    owners = jax.vmap(lambda own: jax.random.permutation(own, N_DP))(jax.random.split(arg_keys[6], 2)).reshape((2, N_DP)).astype(jnp.int32)
    a_factors = centred(arg_keys[7], (FEAT_SHARD, FEAT), 0.5, 3.0, ((0, 32), (1, 8)), jnp.float32)
    g_factors = centred(arg_keys[8], (OUT_WIN, OUT_WIN), 0.5, 3.0, ((0, 32), (1, 8)), jnp.float32)
    return {"activations": activations, "out_grads": out_grads, "a_basis": a_basis, "a_values": a_values, "g_basis": g_basis, "g_values": g_values, "owners": owners, "a_factors": a_factors, "g_factors": g_factors}


decay_rate = 0.5
damping = 0.1

def store_blocks(old_store, fresh, order):
    count = order.shape[0]
    old_blocks = old_store.reshape(count, old_store.shape[0] // count, old_store.shape[1])
    fresh_blocks = fresh.reshape(count, fresh.shape[0] // count, fresh.shape[1])
    mixed = decay_rate * old_blocks[order] + (1.0 - decay_rate) * fresh_blocks
    return old_blocks.at[order].set(mixed).reshape(old_store.shape)

def reference(activations, out_grads, a_basis, a_values, g_basis, g_values, owners, a_factors, g_factors):
    shard = FEAT // N_TENSOR
    basis_blocks = a_basis.reshape(N_TENSOR, shard, shard).astype(jnp.float32)
    grouped_acts = activations.reshape(N_DP, TOK_DEV, FEAT)
    grouped_grads = out_grads.reshape(N_DP, TOK_DEV, OUT_WIN)

    def replica(carry, inputs):
        grad_total, gram_total = carry
        local_acts, local_grads = inputs
        partial_value = jnp.dot(local_grads.T, local_acts, preferred_element_type=jnp.float32).astype(jnp.bfloat16)
        partial_value = lax.optimization_barrier(partial_value).astype(jnp.float32)
        wide = local_acts.astype(jnp.float32).reshape(TOK_DEV, N_TENSOR, shard)
        gram = jnp.einsum('ntf,ntk->ftk', wide, wide)
        return ((grad_total + partial_value, gram_total + gram), None)
    start = (jnp.zeros((OUT_WIN, FEAT), jnp.float32), jnp.zeros((shard, N_TENSOR, shard), jnp.float32))
    (grad_total, gram_total), _ = lax.scan(replica, start, (grouped_acts, grouped_grads))
    grad_sum = lax.optimization_barrier(grad_total.astype(jnp.bfloat16)).astype(jnp.float32)
    grad_eig = jnp.einsum('otf,tfk->otk', grad_sum.reshape(OUT_WIN, N_TENSOR, shard), basis_blocks)
    grad_eig = grad_eig.astype(jnp.bfloat16).reshape(OUT_WIN, FEAT)
    project = jnp.dot(g_basis.T, grad_eig, preferred_element_type=jnp.float32)
    denom = g_values[:, None] * a_values[None, :] + damping
    scaled = project / denom
    kl_total = jnp.sum(project * scaled)
    scaled_low = lax.optimization_barrier(scaled.astype(jnp.bfloat16)).astype(jnp.float32)
    returned = jnp.einsum('itf,tkf->itk', scaled_low.reshape(OUT_WIN, N_TENSOR, shard), basis_blocks)
    returned = returned.astype(jnp.bfloat16).reshape(OUT_WIN, FEAT)
    rows = OUT_WIN // N_DP
    column_blocks = g_basis.reshape(OUT_WIN, N_DP, rows).transpose(1, 0, 2)
    returned_blocks = returned.reshape(N_DP, rows, FEAT)

    def column_block(total, inputs):
        basis_part, returned_part = inputs
        term = jnp.dot(basis_part, returned_part, preferred_element_type=jnp.float32).astype(jnp.bfloat16)
        term = lax.optimization_barrier(term).astype(jnp.float32)
        return (total + term, None)
    precond, _ = lax.scan(column_block, jnp.zeros((OUT_WIN, FEAT), jnp.float32), (column_blocks, returned_blocks))
    update = precond * jnp.sqrt(OUT_WIN * FEAT / kl_total)
    a_fresh = gram_total.reshape(shard, FEAT) / TOKENS
    g_fresh = jnp.dot(out_grads.T, out_grads, preferred_element_type=jnp.float32) / TOKENS
    new_a_factors = store_blocks(a_factors, a_fresh, owners[0])
    new_g_factors = store_blocks(g_factors, g_fresh, owners[1])
    return (update, new_a_factors, new_g_factors)
```

```python
import functools

import jax
import jax.numpy as jnp
from jax import lax
from jax.experimental import pallas as pl
from jax.experimental.pallas import tpu as pltpu
from jax.sharding import PartitionSpec as P

FEAT = 6144
OUT_WIN = 3072
TOKENS = 16384
DECAY = 0.5
DAMPING = 0.1
F32 = jnp.float32
BF16 = jnp.bfloat16
MESH = pl.DeviceIdType.MESH

NZ = 8
CC = 384
CH = 192
OB = 384
GW = 96
AW = 24
GR = 144
GL = 80

NT = (((1,), (1,)), ((), ()))
TN = (((0,), (0,)), ((), ()))


def dot(a, b, dims=(((1,), (0,)), ((), ()))):
    return lax.dot_general(a, b, dims, preferred_element_type=F32)


def add_rows(rows, dst, srcs, step=16):
    def body(i, _):
        at = pl.ds(pl.multiple_of(i * step, step), step)
        total = srcs[0](at).astype(F32)
        for src in srcs[1:]:
            total = total + src(at).astype(F32)
        dst(at, total)
        return 0

    lax.fori_loop(0, rows // step, body, 0, unroll=2)


def store(ref):
    def put(at, value):
        ref[at, :] = value.astype(ref.dtype)

    return put


def load(ref, first=0):
    def get(at):
        return ref[pl.ds(first + at.start, at.size), :]

    return get


def kernel(
    acts, grads, qa, avals, gbasis, gvals, inv, afac, gfac,
    update, new_a, new_g,
    qat, apt, own, csend, crecv, msend, mrecv,
    xsend, xrecv, xown, eg, g4, g4p, gv, gvs, ab, proj, scl,
    bown, bsend, brecv, fsend, frecv,
    gramg, grama, gcs, gcr, gxs, gxr, gown, gsend, grecv,
    klbuf, klz, kly, klx, klc,
    c_s, c_r, m_s, m_r, x_s, x_r, e_s, e_r, b_s, b_r, f_s, f_r,
    gc_s, gc_r, gx_s, gx_r, gz_s, gz_r, g4_s, g4_r, gv_s, gv_r,
    klz_s, klz_r, kly_s, kly_r, klx_s, klx_r, klc_s, klc_r, loc,
):
    dp = lax.axis_index("dp")
    tensor = lax.axis_index("tensor")
    core = dp % 2
    z = (dp // 2) % NZ
    xh = dp // (2 * NZ)
    y = tensor // 2
    xl = tensor % 2

    def dev(xh_=xh, z_=z, core_=core, y_=y, xl_=xl):
        return ((xh_ * NZ + z_) * 2 + core_, y_ * 2 + xl_)

    sibling = dev(core_=1 - core)
    partner = dev(xh_=1 - xh)
    partner_sibling = dev(xh_=1 - xh, core_=1 - core)
    ring = (dev(z_=(z + 1) % NZ), dev(z_=(z + NZ - 1) % NZ))
    pending = []

    def remote(src, dst, ss, rs, to):
        return pltpu.make_async_remote_copy(
            src_ref=src, dst_ref=dst, send_sem=ss, recv_sem=rs, device_id=to, device_id_type=MESH
        )

    def send(*args):
        copy = remote(*args)
        copy.start()
        pending.append(copy)
        return copy

    barrier = pltpu.get_barrier_semaphore()

    def greet(to):
        pl.semaphore_signal(barrier, inc=1, device_id=to, device_id_type=MESH)

    greet(sibling)
    greet(partner)
    greet(partner_sibling)
    for k in range(1, NZ):
        greet(dev(z_=(z + k) % NZ))
    for k in range(1, 4):
        greet(dev(y_=(y + k) % 4))
    greet(dev(xl_=1 - xl))
    greet(dev(xh_=1 - xh, xl_=1 - xl))

    for i in range(6):
        qat[128 * i : 128 * (i + 1), :] = qa[:, 128 * i : 128 * (i + 1)].T
    for i in range(2):
        apt[384 * i : 384 * (i + 1), :] = dot(
            qat[384 * i : 384 * (i + 1), :], acts[...], NT
        ).astype(BF16)

    def chunk(k):
        d = (z + k) % NZ
        block = grads[:, pl.ds(pl.multiple_of(d * OB, 128), OB)]
        theirs = pl.ds(pl.multiple_of((1 - core) * CC, CC), CC)
        csend[d] = dot(apt[theirs, :], block).astype(BF16)
        return d, block

    def chunk_send(d):
        return remote(csend.at[d], crecv.at[d], c_s.at[d], c_r.at[d], sibling)

    def chunk_own(d, block):
        mine = pl.ds(pl.multiple_of(core * CC, CC), CC)
        own[d] = dot(apt[mine, :], block)

    d0, block0 = chunk(4)
    pl.semaphore_wait(barrier, 15)
    pending.append(chunk_send(d0))
    pending[-1].start()
    chunk_own(d0, block0)

    me4 = xh * 2 + core
    gvs[...] = jnp.broadcast_to(gvals[...].reshape(1, GW), gvs.shape)
    keep_g = pltpu.make_async_copy(gbasis, g4.at[pl.ds(pl.multiple_of(me4 * GW, GW), GW)], loc.at[0])
    keep_v = pltpu.make_async_copy(gvs, gv.at[me4], loc.at[1])
    keep_g.start()
    keep_v.start()
    send(gbasis, g4.at[pl.ds(pl.multiple_of(me4 * GW, GW), GW)], g4_s.at[0], g4_r.at[0], partner)
    send(gvs, gv.at[me4], gv_s.at[0], gv_r.at[0], partner)
    send(gvs, gv.at[me4], gv_s.at[1], gv_r.at[1], sibling)
    send(gvs, gv.at[me4], gv_s.at[2], gv_r.at[2], partner_sibling)

    def offset(direction, it):
        k = 4 - it
        return k if direction == 0 else (NZ - k) % NZ

    def ring_step(it, parity, own_half, sbuf, rbuf, ss, rs, sizes):
        if parity == 1 and it == 0:
            return
        for direction in range(2):
            half = parity if direction == 0 else 1 - parity
            size = sizes[half]
            d = (z + offset(direction, it)) % NZ
            srcs = list(own_half(d, half))
            rows = pl.ds(0, size)
            if it > parity:
                before = rbuf.at[direction, half, it - 1, rows]
                remote(
                    before, before, ss.at[direction, half, it - 1],
                    rs.at[direction, half, it - 1], ring[direction],
                ).wait_recv()
                srcs.append(load(rbuf.at[direction, half, it - 1]))
            add_rows(size, store(sbuf.at[direction, half, it]), srcs)
            send(
                sbuf.at[direction, half, it, rows], rbuf.at[direction, half, it, rows],
                ss.at[direction, half, it], rs.at[direction, half, it], ring[direction],
            )

    def ring_last(half, rbuf, ss, rs, sizes):
        rows = pl.ds(0, sizes[half])
        for direction in range(2):
            last = rbuf.at[direction, half, 3, rows]
            remote(
                last, last, ss.at[direction, half, 3], rs.at[direction, half, 3], ring[direction]
            ).wait_recv()
        return [load(rbuf.at[0, half, 3]), load(rbuf.at[1, half, 3])]

    main_sizes = (CH, CH)
    back_sizes = (CH // 2, CH // 2)
    gram_sizes = (GL, GR - GL)

    def main_own(d, half):
        return load(own.at[d], half * CH), load(crecv.at[d], half * CH)

    def main_step(it, parity):
        ring_step(it, parity, main_own, msend, mrecv, m_s, m_r, main_sizes)

    def main_chunks(ks):
        for k in ks:
            d, block = chunk(k)
            pending.append(chunk_send(d))
            pending[-1].start()
            chunk_own(d, block)

    def main_wait(ks):
        for k in ks:
            chunk_send((z + k) % NZ).wait_recv()

    def gram_g(first, last):
        mine = grads[:, pl.ds(pl.multiple_of(tensor * OB, 128), OB)]

        def body(i, _):
            at = pl.multiple_of(i * 384, 128)
            part = dot(grads[:, pl.ds(at, 384)], mine, TN)
            gramg[pl.ds(i * 4, 4)] = part.reshape(4, GW, OB)
            return 0

        lax.fori_loop(first, last, body, 0)

    def gram_a():
        def body(i, _):
            at = pl.multiple_of(i * 384, 128)
            part = dot(acts[:, pl.ds(at, 384)], acts[...], TN)
            grama[pl.ds(i * 16, 16)] = part.reshape(16, AW, 2 * CC)
            return 0

        lax.fori_loop(0, 2, body, 0)

    def gram_block(xh_, z_, core_):
        w = (xh_ * NZ + z_) * 2 + core_
        return gramg[inv[1, w]], grama[inv[0, w]]

    def put_block(ref, g_part, a_part):
        ref[0:GW, :] = g_part.astype(ref.dtype)
        tail = jnp.concatenate([a_part[:, 0:384], a_part[:, 384:768]], axis=0)
        ref[GW:GR, :] = tail.astype(ref.dtype)

    def gram_core():
        for turn in range(2):
            other = 1 - xh if turn == 0 else xh

            def body(i, _):
                put_block(gcs.at[turn, i], *gram_block(other, i, 1 - core))
                return 0

            lax.fori_loop(0, NZ, body, 0)
            send(gcs.at[turn], gcr.at[turn], gc_s.at[turn], gc_r.at[turn], sibling)

    def gram_sum(dst, xh_, others):
        def body(i, _):
            put_block(gown.at[i], *gram_block(xh_, i, core))
            add_rows(GR, store(dst.at[i]), [load(gown.at[i])] + [load(o.at[i]) for o in others])
            return 0

        lax.fori_loop(0, NZ, body, 0)

    def gram_x():
        remote(gcs.at[0], gcr.at[0], gc_s.at[0], gc_r.at[0], sibling).wait_recv()
        gram_sum(gxs, 1 - xh, [gcr.at[0]])
        send(gxs, gxr, gx_s.at[0], gx_r.at[0], partner)

    def gram_own():
        remote(gcs.at[1], gcr.at[1], gc_s.at[1], gc_r.at[1], sibling).wait_recv()
        remote(gxs, gxr, gx_s.at[0], gx_r.at[0], partner).wait_recv()
        gram_sum(gown, xh, [gcr.at[1], gxr])

    def gram_half(d, half):
        return (load(gown.at[d], half * GL),)

    def gram_step(it, parity):
        ring_step(it, parity, gram_half, gsend, grecv, gz_s, gz_r, gram_sizes)

    main_chunks((3, 5))
    main_wait((4,))
    main_step(0, 0)
    main_wait((3, 5))
    main_step(1, 1)
    main_chunks((2, 6))
    gram_g(0, 4)
    main_step(1, 0)
    main_wait((2, 6))
    main_step(2, 1)
    main_chunks((1, 7, 0))
    gram_g(4, 8)
    main_step(2, 0)
    main_wait((1, 7, 0))
    main_step(3, 1)
    gram_a()
    gram_core()
    main_step(3, 0)
    gram_x()
    send(gbasis, g4.at[pl.ds(pl.multiple_of(me4 * GW, GW), GW)], g4_s.at[1], g4_r.at[1], sibling)
    p_partner = (1 - xh) * 2 + core
    remote(gbasis, g4.at[pl.ds(pl.multiple_of(me4 * GW, GW), GW)], g4_s.at[0], g4_r.at[0], partner).wait_recv()
    piece = g4.at[pl.ds(pl.multiple_of(p_partner * GW, GW), GW)]
    send(piece, piece, g4_s.at[2], g4_r.at[2], sibling)
    ab[...] = jnp.broadcast_to(avals[...].reshape(1, 2 * CC), (128, 2 * CC)).T

    def main_last(half_static):
        return ring_last(half_static, mrecv, m_s, m_r, main_sizes)

    main_last(0)
    main_last(1)

    def half_srcs(half):
        at = pl.multiple_of(half * CH, CH)
        return [
            load(own.at[z], at), load(crecv.at[z], at),
            load(mrecv.at[0, half, 3]), load(mrecv.at[1, half, 3]),
        ]

    add_rows(CH, store(xsend), half_srcs(1 - xh))
    send(xsend, xrecv, x_s.at[0], x_r.at[0], partner)
    add_rows(CH, store(xown), half_srcs(xh))
    gram_own()
    remote(xsend, xrecv, x_s.at[0], x_r.at[0], partner).wait_recv()
    add_rows(CH, store(eg.at[z]), [load(xown), load(xrecv)])

    HALF = CH // 2

    def gather_copy(direction, half, it):
        b = (z + NZ - it) % NZ if direction == 0 else (z + it) % NZ
        part = eg.at[b, pl.ds(half * HALF, HALF)]
        return remote(
            part, part, e_s.at[direction, half, it], e_r.at[direction, half, it], ring[direction]
        )

    def gather_start(it):
        for half in (0, 1):
            for direction in (0, 1):
                side = half if direction == 0 else 1 - half
                if half == 1 and it == 3:
                    continue
                if it > 0:
                    gather_copy(direction, side, it - 1).wait_recv()
                copy = gather_copy(direction, side, it)
                copy.start()
                pending.append(copy)

    def project(b, first=False):
        part = dot(eg[b], g4[:, pl.ds(pl.multiple_of(b * OB, 128), OB)], NT)
        proj[...] = part if first else proj[...] + part

    gather_start(0)
    gram_step(0, 0)
    gram_step(1, 1)
    keep_g.wait()
    keep_v.wait()
    remote(gbasis, g4.at[pl.ds(pl.multiple_of(me4 * GW, GW), GW)], g4_s.at[1], g4_r.at[1], sibling).wait_recv()
    remote(piece, piece, g4_s.at[2], g4_r.at[2], sibling).wait_recv()
    project(z, True)
    gather_start(1)
    for i in range(NZ):
        for h in range(2):
            to = i * OB + h * CH
            at = h * (OUT_WIN // 2) + i * CH
            g4p[:, to : to + CH] = g4[:, at : at + CH]
    gram_step(1, 0)
    project((z + 1) % NZ)
    project((z + 7) % NZ)
    gather_start(2)
    gram_step(2, 1)
    project((z + 2) % NZ)
    project((z + 6) % NZ)
    gather_start(3)
    gather_copy(0, 1, 2).wait_recv()
    gather_copy(1, 0, 2).wait_recv()
    project((z + 3) % NZ)
    project((z + 5) % NZ)
    gather_copy(0, 0, 3).wait_recv()
    gather_copy(1, 1, 3).wait_recv()
    project((z + 4) % NZ)

    remote(gvs, gv.at[me4], gv_s.at[0], gv_r.at[0], partner).wait_recv()
    remote(gvs, gv.at[me4], gv_s.at[1], gv_r.at[1], sibling).wait_recv()
    remote(gvs, gv.at[me4], gv_s.at[2], gv_r.at[2], partner_sibling).wait_recv()
    j = core * 2 + xh
    g_row = jnp.concatenate([gv[p, 0:1, :] for p in range(4)], axis=1)

    def scale(i, kl):
        at = pl.multiple_of(i * 16, 16)
        value = proj[pl.ds(at, 16), :]
        a_col = ab[pl.ds(pl.multiple_of(j * CH + at, 16), 16), 0:1]
        scaled = value / (a_col * g_row + DAMPING)
        scl[pl.ds(at, 16), :] = scaled.astype(BF16)
        return kl + value * scaled

    kl = lax.fori_loop(0, CH // 16, scale, jnp.zeros((16, OB), F32))
    klbuf[0] = jnp.full((8, 128), jnp.sum(kl), F32)

    def kl_round(stage, count, place, peer, buf, ss, rs):
        out = []
        for k in range(1, count):
            copy = remote(klbuf.at[stage], buf.at[place(0)], ss.at[k], rs.at[place(0)], peer(k))
            copy.start()
            pending.append(copy)
            out.append(
                lambda k=k: remote(
                    klbuf.at[stage], buf.at[place(k)], ss.at[k], rs.at[place(k)], peer(k)
                )
            )

        def finish():
            total = klbuf[stage]
            for k in range(1, count):
                out[k - 1]().wait_recv()
                total = total + buf[place(k)]
            klbuf[stage + 1] = total

        return finish

    kl_z = kl_round(
        0, NZ, lambda k: (z + k) % NZ, lambda k: dev(z_=(z + k) % NZ), klz, klz_s, klz_r
    )

    def back_chunk(k):
        d = (z + k) % NZ
        bown[d] = dot(scl[...], g4p[:, pl.ds(pl.multiple_of(d * OB, 128), OB)])

    def back_own(d, half):
        return (load(bown.at[d], half * HALF),)

    def back_step(it, parity):
        ring_step(it, parity, back_own, bsend, brecv, b_s, b_r, back_sizes)

    back_chunk(4)
    back_step(0, 0)
    back_chunk(3)
    back_chunk(5)
    back_step(1, 1)
    back_chunk(2)
    back_chunk(6)
    back_step(1, 0)
    back_step(2, 1)
    kl_z()
    kl_y = kl_round(
        1, 4, lambda k: (y + k) % 4, lambda k: dev(y_=(y + k) % 4), kly, kly_s, kly_r
    )
    gram_step(2, 0)
    back_chunk(1)
    back_chunk(7)
    back_step(2, 0)
    back_step(3, 1)
    kl_y()
    x_at = xh * 2 + xl
    kl_x = kl_round(
        2, 4,
        lambda k: (xh ^ (k // 2)) * 2 + (xl ^ (k % 2)),
        lambda k: dev(xh_=xh ^ (k // 2), xl_=xl ^ (k % 2)),
        klx, klx_s, klx_r,
    )
    back_chunk(0)
    back_step(3, 0)
    gram_step(3, 1)
    gram_step(3, 0)
    kl_x()
    kl_c = kl_round(
        3, 2, lambda k: core if k == 0 else 1 - core, lambda k: sibling, klc, klc_s, klc_r
    )

    for half in (0, 1):
        srcs = ring_last(half, brecv, b_s, b_r, back_sizes)
        srcs.append(load(bown.at[z], half * HALF))
        at = half * HALF
        add_rows(HALF, store(xown.at[pl.ds(at, HALF)]), srcs)
    turned = xown[...].T.astype(BF16)
    for p in range(4):
        fsend[p] = turned[p * GW : (p + 1) * GW, :]
    mine4 = pltpu.make_async_copy(fsend.at[me4], frecv.at[j], loc.at[2])
    mine4.start()
    places = (
        (sibling, xh * 2 + 1 - core, (1 - core) * 2 + xh),
        (partner, (1 - xh) * 2 + core, core * 2 + 1 - xh),
        (partner_sibling, (1 - xh) * 2 + 1 - core, (1 - core) * 2 + 1 - xh),
    )
    for n in (1, 2, 0):
        to, p, _ = places[n]
        send(fsend.at[p], frecv.at[j], f_s.at[n], f_r.at[n], to)

    for half in (0, 1):
        srcs = ring_last(half, grecv, gz_s, gz_r, gram_sizes)
        srcs.append(load(gown.at[z], half * GL))
        at = half * GL
        size = gram_sizes[half]
        add_rows(size, store(gown.at[(z + 1) % NZ, pl.ds(at, size)]), srcs)
    fresh = (1.0 - DECAY) / TOKENS
    last = gown.at[(z + 1) % NZ]
    new_g[...] = DECAY * gfac[...] + fresh * last[0:GW, :]
    new_a[:, 0:384] = DECAY * afac[:, 0:384] + fresh * last[GW : GW + AW, :]
    new_a[:, 384:768] = DECAY * afac[:, 384:768] + fresh * last[GW + AW : GR, :]

    kl_c()
    gain = jnp.sqrt(OUT_WIN * FEAT / klbuf[4, 0:1, 0:1])
    mine4.wait()
    for n in (0, 1, 2):
        to, p, slot = places[n]
        remote(fsend.at[p], frecv.at[slot], f_s.at[n], f_r.at[n], to).wait_recv()
    total = dot(frecv[0], qat[0:CH, :])
    for i in range(1, 4):
        total = total + dot(frecv[i], qat[i * CH : (i + 1) * CH, :])
    update[...] = total * gain

    for copy in pending:
        copy.wait_send()


def per_device(
    activations, out_grads, a_basis, a_values, g_basis, g_values, owners, a_factors, g_factors
):
    workers = jnp.arange(owners.shape[1], dtype=jnp.int32)
    inverse = jnp.sum(
        jnp.where(owners[:, None, :] == workers[None, :, None], workers[None, None, :], 0), axis=2
    )
    vmem = pl.BlockSpec(memory_space=pltpu.VMEM)
    smem = pl.BlockSpec(memory_space=pltpu.SMEM)
    sem = pltpu.SemaphoreType.DMA
    v = pltpu.VMEM
    scratch = [
        v((768, 768), BF16), v((768, 512), BF16), v((NZ, CC, OB), F32),
        v((NZ, CC, OB), BF16), v((NZ, CC, OB), BF16),
        v((2, 2, 4, CH, OB), BF16), v((2, 2, 4, CH, OB), BF16),
        v((CH, OB), BF16), v((CH, OB), BF16), v((CH, OB), F32),
        v((NZ, CH, OB), BF16), v((4 * GW, OUT_WIN), BF16), v((4 * GW, OUT_WIN), BF16), v((4, 8, GW), F32), v((8, GW), F32),
        v((768, 128), F32), v((CH, OB), F32), v((CH, OB), BF16),
        v((NZ, CH, OB), F32), v((2, 2, 4, CH // 2, OB), BF16), v((2, 2, 4, CH // 2, OB), BF16),
        v((4, GW, CH), BF16), v((4, GW, CH), BF16),
        v((32, GW, OB), F32), v((32, AW, 768), F32),
        v((2, NZ, GR, OB), BF16), v((2, NZ, GR, OB), BF16),
        v((NZ, GR, OB), BF16), v((NZ, GR, OB), BF16), v((NZ, GR, OB), F32),
        v((2, 2, 4, GL, OB), BF16), v((2, 2, 4, GL, OB), BF16),
        v((5, 8, 128), F32), v((NZ, 8, 128), F32), v((4, 8, 128), F32), v((4, 8, 128), F32),
        v((2, 8, 128), F32),
        sem((NZ,)), sem((NZ,)), sem((2, 2, 4)), sem((2, 2, 4)), sem((1,)), sem((1,)),
        sem((2, 2, 4)), sem((2, 2, 4)), sem((2, 2, 4)), sem((2, 2, 4)), sem((3,)), sem((3,)),
        sem((2,)), sem((2,)), sem((1,)), sem((1,)), sem((2, 2, 4)), sem((2, 2, 4)),
        sem((3,)), sem((3,)), sem((3,)), sem((3,)),
        sem((NZ,)), sem((NZ,)), sem((4,)), sem((4,)), sem((4,)), sem((4,)), sem((2,)), sem((2,)),
        sem((3,)),
    ]
    return pl.pallas_call(
        kernel,
        out_shape=(
            jax.ShapeDtypeStruct((GW, 768), F32),
            jax.ShapeDtypeStruct((AW, 768), F32),
            jax.ShapeDtypeStruct((GW, OB), F32),
        ),
        in_specs=[vmem] * 6 + [smem] + [vmem] * 2,
        out_specs=(vmem, vmem, vmem),
        scratch_shapes=scratch,
        compiler_params=pltpu.CompilerParams(
            collective_id=0, has_side_effects=True, vmem_limit_bytes=60 << 20
        ),
        cost_estimate=pl.CostEstimate(
            flops=5_400_000_000, bytes_accessed=8_000_000, transcendentals=0
        ),
        name="precondition",
    )(
        activations, out_grads, a_basis, a_values, g_basis.T,
        g_values, inverse, a_factors, g_factors,
    )


def solution(mesh):
    in_specs = (
        P("dp", "tensor"),
        P("dp", None),
        P("tensor", None),
        P("tensor"),
        P(None, "dp"),
        P("dp"),
        P(),
        P("dp", "tensor"),
        P("dp", "tensor"),
    )
    out_specs = (P("dp", "tensor"), P("dp", "tensor"), P("dp", "tensor"))
    return jax.shard_map(
        per_device, mesh=mesh, in_specs=in_specs, out_specs=out_specs, check_vma=False
    )
```

```python
import functools

import jax
import jax.numpy as jnp
from jax import lax
from jax.experimental import pallas as pl
from jax.experimental.pallas import tpu as pltpu
from jax.sharding import PartitionSpec as P

FEAT = 6144
OUT_WIN = 3072
TOKENS = 16384
DECAY = 0.5
DAMPING = 0.1
F32 = jnp.float32
BF16 = jnp.bfloat16
MESH = pl.DeviceIdType.MESH

NZ = 8
CC = 384
HALF = 192
CH = 96
OB = 384
GW = 96
AW = 24
GR = 144
GL = 80

NT = (((1,), (1,)), ((), ()))
TN = (((0,), (0,)), ((), ()))


def dot(a, b, dims=(((1,), (0,)), ((), ()))):
    return lax.dot_general(a, b, dims, preferred_element_type=F32)


def add_rows(rows, dst, srcs, step=16):
    def body(i, _):
        at = pl.ds(pl.multiple_of(i * step, step), step)
        total = srcs[0](at).astype(F32)
        for src in srcs[1:]:
            total = total + src(at).astype(F32)
        dst(at, total)
        return 0

    lax.fori_loop(0, rows // step, body, 0, unroll=2)


def store(ref):
    def put(at, value):
        ref[at, :] = value.astype(ref.dtype)

    return put


def load(ref, first=0):
    def get(at):
        return ref[pl.ds(first + at.start, at.size), :]

    return get


def kernel(
    acts_in, grads_in, qa_in, gbasis_in, avals, gvals, inv,
    total, gram, gain,
    acts, grads, qa, qat, apt, own, csend, crecv,
    asend, arecv, xsend, xrecv, xown, xbs, xbr, bsend, brecv,
    eg, g4, g4p, gv, gvs, ab, proj, scl,
    rown, rsend, rrecv, fsend, frecv,
    gramg, grama, gcs, gcr, gxs, gxr, gown, gsend, grecv,
    klbuf, klz, kly, klx, klc,
    c_s, c_r, a_s, a_r, x_s, x_r, xb_s, xb_r, b_s, b_r, e_s, e_r, r_s, r_r, f_s, f_r,
    gc_s, gc_r, gx_s, gx_r, gz_s, gz_r, gb_s, gb_r, gv_s, gv_r,
    klz_s, klz_r, kly_s, kly_r, klx_s, klx_r, klc_s, klc_r, loc,
):
    dp = lax.axis_index("dp")
    tensor = lax.axis_index("tensor")
    core = dp % 2
    z = (dp // 2) % NZ
    xh = dp // (2 * NZ)
    y = tensor // 2
    xl = tensor % 2

    def dev(xh_=xh, z_=z, core_=core, y_=y, xl_=xl):
        return ((xh_ * NZ + z_) * 2 + core_, y_ * 2 + xl_)

    sibling = dev(core_=1 - core)
    partner = dev(xh_=1 - xh)
    partner_sibling = dev(xh_=1 - xh, core_=1 - core)
    ring = (dev(z_=(z + 1) % NZ), dev(z_=(z + NZ - 1) % NZ))
    pending = []

    def remote(src, dst, ss, rs, to):
        return pltpu.make_async_remote_copy(
            src_ref=src, dst_ref=dst, send_sem=ss, recv_sem=rs, device_id=to, device_id_type=MESH
        )

    def send(*args):
        copy = remote(*args)
        copy.start()
        pending.append(copy)
        return copy

    def drain():
        for copy in pending:
            copy.wait_send()
        pending.clear()

    barrier = pltpu.get_barrier_semaphore()

    def greet(to):
        pl.semaphore_signal(barrier, inc=1, device_id=to, device_id_type=MESH)

    me4 = xh * 2 + core
    mine4 = pl.ds(pl.multiple_of(me4 * GW, GW), GW)
    loads = [
        pltpu.make_async_copy(qa_in, qa, loc.at[0]),
        pltpu.make_async_copy(acts_in, acts, loc.at[1]),
        pltpu.make_async_copy(grads_in, grads, loc.at[2]),
        pltpu.make_async_copy(gbasis_in, g4.at[mine4], loc.at[3]),
    ]
    for copy in loads:
        copy.start()
    greet(sibling)
    greet(partner)
    greet(partner_sibling)
    for k in range(1, NZ):
        greet(dev(z_=(z + k) % NZ))
    for k in range(1, 4):
        greet(dev(y_=(y + k) % 4))
    greet(dev(xl_=1 - xl))
    greet(dev(xh_=1 - xh, xl_=1 - xl))

    loads[0].wait()
    for i in range(6):
        qat[128 * i : 128 * (i + 1), :] = qa[:, 128 * i : 128 * (i + 1)].T
    loads[1].wait()
    for i in range(2):
        apt[384 * i : 384 * (i + 1), :] = dot(
            qat[384 * i : 384 * (i + 1), :], acts[...], NT
        ).astype(BF16)
    loads[2].wait()

    def chunk(k):
        d = (z + k) % NZ
        block = grads[:, pl.ds(pl.multiple_of(d * OB, 128), OB)]
        theirs = pl.ds(pl.multiple_of((1 - core) * CC, CC), CC)
        csend[d] = dot(apt[theirs, :], block).astype(BF16)
        return d, block

    def chunk_send(d):
        return remote(csend.at[d], crecv.at[d], c_s.at[d], c_r.at[d], sibling)

    def chunk_own(d, block):
        mine = pl.ds(pl.multiple_of(core * CC, CC), CC)
        own[d] = dot(apt[mine, :], block)

    d0, block0 = chunk(4)
    loads[3].wait()
    gvs[...] = jnp.broadcast_to(gvals[...].reshape(1, GW), gvs.shape)
    pl.semaphore_wait(barrier, 15)
    pending.append(chunk_send(d0))
    pending[-1].start()

    quarter = OUT_WIN // 4

    def gb_part(p, y_):
        rows = pl.ds(pl.multiple_of(p * GW, GW), GW)
        return g4.at[rows, pl.ds(pl.multiple_of(y_ * quarter, 128), quarter)]

    def gb_all(p):
        return g4.at[pl.ds(pl.multiple_of(p * GW, GW), GW)]

    p_partner = (1 - xh) * 2 + core
    send(gb_part(me4, y), gb_part(me4, y), gb_s.at[0], gb_r.at[y], partner)
    chunk_own(d0, block0)

    def offset(direction, it):
        k = 4 - it
        return k if direction == 0 else (NZ - k) % NZ

    def ring_step(it, parity, own_half, sbuf, rbuf, ss, rs, sizes):
        for direction in range(2):
            half = parity if direction == 0 else 1 - parity
            size = sizes[half]
            d = (z + offset(direction, it)) % NZ
            srcs = list(own_half(d, half))
            rows = pl.ds(0, size)
            if it > parity:
                before = rbuf.at[direction, half, it - 1, rows]
                remote(
                    before, before, ss.at[direction, half, it - 1],
                    rs.at[direction, half, it - 1], ring[direction],
                ).wait_recv()
                srcs.append(load(rbuf.at[direction, half, it - 1]))
            add_rows(size, store(sbuf.at[direction, half, it]), srcs)
            send(
                sbuf.at[direction, half, it, rows], rbuf.at[direction, half, it, rows],
                ss.at[direction, half, it], rs.at[direction, half, it], ring[direction],
            )

    def ring_last(half, rbuf, ss, rs, sizes):
        rows = pl.ds(0, sizes[half])
        for direction in range(2):
            last = rbuf.at[direction, half, 3, rows]
            remote(
                last, last, ss.at[direction, half, 3], rs.at[direction, half, 3], ring[direction]
            ).wait_recv()
        return [load(rbuf.at[0, half, 3]), load(rbuf.at[1, half, 3])]

    a_sizes = (CH, CH)
    part_sizes = (CH // 2, CH // 2)
    gram_sizes = (GL, GR - GL)
    PART = CH // 2

    def chunks(ks):
        for k in ks:
            d, block = chunk(k)
            pending.append(chunk_send(d))
            pending[-1].start()
            chunk_own(d, block)

    def chunks_wait(ks):
        for k in ks:
            chunk_send((z + k) % NZ).wait_recv()

    def a_own(d, half):
        return load(own.at[d], half * CH), load(crecv.at[d], half * CH)

    def a_step(it, parity):
        ring_step(it, parity, a_own, asend, arecv, a_s, a_r, a_sizes)

    def bx_copy(d):
        return remote(xbs.at[d], xbr.at[d], xb_s.at[d], xb_r.at[d], partner)

    def bx_send(ks):
        for k in ks:
            d = (z + k) % NZ
            at = HALF + (1 - xh) * CH
            add_rows(CH, store(xbs.at[d]), [load(own.at[d], at), load(crecv.at[d], at)])
            copy = bx_copy(d)
            copy.start()
            pending.append(copy)

    def bx_wait(ks):
        for k in ks:
            bx_copy((z + k) % NZ).wait_recv()

    def b_own(d, half):
        at = HALF + xh * CH + half * PART
        return load(own.at[d], at), load(crecv.at[d], at), load(xbr.at[d], half * PART)

    def b_step(it, parity):
        ring_step(it, parity, b_own, bsend, brecv, b_s, b_r, part_sizes)

    def gram_g(first, last):
        mine = grads[:, pl.ds(pl.multiple_of(tensor * OB, 128), OB)]

        def body(i, _):
            at = pl.multiple_of(i * 384, 128)
            part = dot(grads[:, pl.ds(at, 384)], mine, TN)
            gramg[pl.ds(i * 4, 4)] = part.reshape(4, GW, OB)
            return 0

        lax.fori_loop(first, last, body, 0)

    def gram_a():
        def body(i, _):
            at = pl.multiple_of(i * 384, 128)
            part = dot(acts[:, pl.ds(at, 384)], acts[...], TN)
            grama[pl.ds(i * 16, 16)] = part.reshape(16, AW, 2 * CC)
            return 0

        lax.fori_loop(0, 2, body, 0)

    def gram_block(xh_, z_, core_):
        w = (xh_ * NZ + z_) * 2 + core_
        return gramg[inv[1, w]], grama[inv[0, w]]

    def put_block(ref, g_part, a_part):
        ref[0:GW, :] = g_part.astype(ref.dtype)
        tail = jnp.concatenate([a_part[:, 0:384], a_part[:, 384:768]], axis=0)
        ref[GW:GR, :] = tail.astype(ref.dtype)

    def gram_core(turn):
        other = 1 - xh if turn == 0 else xh

        def body(i, _):
            put_block(gcs.at[turn, i], *gram_block(other, i, 1 - core))
            return 0

        lax.fori_loop(0, NZ, body, 0)
        send(gcs.at[turn], gcr.at[turn], gc_s.at[turn], gc_r.at[turn], sibling)

    def gram_sum(dst, xh_, others):
        def body(i, _):
            put_block(gown.at[i], *gram_block(xh_, i, core))
            add_rows(GR, store(dst.at[i]), [load(gown.at[i])] + [load(o.at[i]) for o in others])
            return 0

        lax.fori_loop(0, NZ, body, 0)

    def gram_x():
        remote(gcs.at[0], gcr.at[0], gc_s.at[0], gc_r.at[0], sibling).wait_recv()
        gram_sum(gxs, 1 - xh, [gcr.at[0]])
        send(gxs, gxr, gx_s.at[0], gx_r.at[0], partner)

    def gram_own():
        remote(gcs.at[1], gcr.at[1], gc_s.at[1], gc_r.at[1], sibling).wait_recv()
        remote(gxs, gxr, gx_s.at[0], gx_r.at[0], partner).wait_recv()
        gram_sum(gown, xh, [gcr.at[1], gxr])

    def gram_half(d, half):
        return (load(gown.at[d], half * GL),)

    def gram_step(it, parity):
        ring_step(it, parity, gram_half, gsend, grecv, gz_s, gz_r, gram_sizes)

    def gather_copy(s, direction, half, it):
        b = (z + NZ - it) % NZ if direction == 0 else (z + it) % NZ
        part = eg.at[s, b, pl.ds(half * PART, PART)]
        return remote(
            part, part, e_s.at[s, direction, half, it], e_r.at[s, direction, half, it],
            ring[direction],
        )

    def gather(s, it):
        for half in (0, 1):
            for direction in (0, 1):
                side = half if direction == 0 else 1 - half
                if half == 1 and it == 3:
                    continue
                if it > 0:
                    gather_copy(s, direction, side, it - 1).wait_recv()
                copy = gather_copy(s, direction, side, it)
                copy.start()
                pending.append(copy)

    def gather_last(s):
        gather_copy(s, 0, 1, 2).wait_recv()
        gather_copy(s, 1, 0, 2).wait_recv()
        project(s, 3)
        project(s, 5)
        gather_copy(s, 0, 0, 3).wait_recv()
        gather_copy(s, 1, 1, 3).wait_recv()
        project(s, 4)

    def project(s, k):
        b = (z + k) % NZ
        part = dot(eg[s, b], g4[:, pl.ds(pl.multiple_of(b * OB, 128), OB)], NT)
        proj[s] = part if k == 0 else proj[s] + part

    def scale(s):
        g_row = jnp.concatenate([gv[p, 0:1, :] for p in range(4)], axis=1)
        first = core * CC + s * HALF + xh * CH

        def body(i, kl):
            at = pl.multiple_of(i * 16, 16)
            value = proj[s, pl.ds(at, 16), :]
            a_col = ab[pl.ds(pl.multiple_of(first + at, 16), 16), 0:1]
            scaled = value / (a_col * g_row + DAMPING)
            scl[s, pl.ds(at, 16), :] = scaled.astype(BF16)
            return kl + value * scaled

        return lax.fori_loop(0, CH // 16, body, jnp.zeros((16, OB), F32))

    def back_chunks(s, ks):
        for k in ks:
            d = (z + k) % NZ
            rown[s, d] = dot(scl[s], g4p[:, pl.ds(pl.multiple_of(d * OB, 128), OB)])

    def back_step(s, it, parity):
        def back_own(d, half):
            return (load(rown.at[s, d], half * PART),)

        ring_step(
            it, parity, back_own, rsend.at[s], rrecv.at[s], r_s.at[s], r_r.at[s], part_sizes
        )

    places = (
        (sibling, xh * 2 + 1 - core, (1 - core) * 2 + xh),
        (partner, (1 - xh) * 2 + core, core * 2 + 1 - xh),
        (partner_sibling, (1 - xh) * 2 + 1 - core, (1 - core) * 2 + 1 - xh),
    )
    j = core * 2 + xh

    def final_copy(s, n):
        to, p, _ = places[n]
        return remote(fsend.at[s, p], frecv.at[s, j], f_s.at[s, n], f_r.at[s, n], to)

    def final_keep(s):
        return pltpu.make_async_copy(fsend.at[s, me4], frecv.at[s, j], loc.at[4 + s])

    def final_send(s):
        for half in (0, 1):
            srcs = ring_last(half, rrecv.at[s], r_s.at[s], r_r.at[s], part_sizes)
            srcs.append(load(rown.at[s, z], half * PART))
            add_rows(PART, store(xown.at[pl.ds(half * PART, PART)]), srcs)
        turned = xown[...].T.astype(BF16)
        for p in range(4):
            fsend[s, p] = turned[p * GW : (p + 1) * GW, :]
        for n in (1, 2, 0):
            copy = final_copy(s, n)
            copy.start()
            pending.append(copy)
        final_keep(s).start()

    def final_dot(s):
        final_keep(s).wait()
        for n in (0, 1, 2):
            to, p, slot = places[n]
            remote(
                fsend.at[s, p], frecv.at[s, slot], f_s.at[s, n], f_r.at[s, n], to
            ).wait_recv()
        out = None
        for i in range(4):
            first = (i // 2) * CC + s * HALF + (i % 2) * CH
            part = dot(frecv[s, i], qat[first : first + CH, :])
            out = part if out is None else out + part
        return out

    def kl_round(stage, count, place, peer, buf, ss, rs):
        copies = []
        for k in range(1, count):
            send(klbuf.at[stage], buf.at[place(0)], ss.at[k], rs.at[place(0)], peer(k))
            copies.append(
                remote(klbuf.at[stage], buf.at[place(k)], ss.at[k], rs.at[place(k)], peer(k))
            )

        def finish():
            value = klbuf[stage]
            for k in range(1, count):
                copies[k - 1].wait_recv()
                value = value + buf[place(k)]
            klbuf[stage + 1] = value

        return finish

    chunks((3, 5))
    chunks_wait((4,))
    a_step(0, 0)
    chunks_wait((3, 5))
    a_step(1, 1)
    bx_send((4, 3, 5))
    chunks((2, 6))
    a_step(1, 0)
    chunks_wait((2, 6))
    bx_send((2, 6))
    chunks((1, 7, 0))
    a_step(2, 1)
    chunks_wait((1, 7, 0))
    bx_send((1, 7, 0))
    remote(gb_part(p_partner, y), gb_part(p_partner, y), gb_s.at[0], gb_r.at[y], partner).wait_recv()
    for k in range(1, 4):
        send(
            gb_part(p_partner, y), gb_part(p_partner, y), gb_s.at[k], gb_r.at[y],
            dev(y_=(y + k) % 4),
        )
    send(gb_all(me4), gb_all(me4), gb_s.at[4], gb_r.at[4], sibling)
    others = (sibling, partner, partner_sibling)
    for n in range(3):
        send(gvs, gv.at[me4], gv_s.at[n], gv_r.at[n], others[n])
    gram_g(0, 2)
    a_step(2, 0)
    gram_g(2, 4)
    a_step(3, 1)
    gram_g(4, 6)
    a_step(3, 0)
    bx_wait((4, 3, 5))
    b_step(0, 0)
    b_step(1, 1)
    gram_g(6, 8)
    gram_a()

    for half in (0, 1):
        ring_last(half, arecv, a_s, a_r, a_sizes)

    def a_srcs(half):
        at = pl.multiple_of(half * CH, CH)
        return [
            load(own.at[z], at), load(crecv.at[z], at),
            load(arecv.at[0, half, 3]), load(arecv.at[1, half, 3]),
        ]

    add_rows(CH, store(xsend), a_srcs(1 - xh))
    send(xsend, xrecv, x_s.at[0], x_r.at[0], partner)
    add_rows(CH, store(xown), a_srcs(xh))
    b_step(1, 0)
    gram_core(0)
    gram_core(1)
    bx_wait((2, 6))
    b_step(2, 1)
    remote(xsend, xrecv, x_s.at[0], x_r.at[0], partner).wait_recv()
    add_rows(CH, store(eg.at[0, z]), [load(xown), load(xrecv)])
    gather(0, 0)
    b_step(2, 0)
    gram_x()
    bx_wait((1, 7, 0))
    b_step(3, 1)
    for k in range(1, 4):
        there = gb_part(p_partner, (y + k) % 4)
        remote(there, there, gb_s.at[k], gb_r.at[(y + k) % 4], dev(y_=(y + k) % 4)).wait_recv()
    send(gb_all(p_partner), gb_all(p_partner), gb_s.at[5], gb_r.at[5], sibling)
    gather(0, 1)
    b_step(3, 0)
    loc_ab = jnp.broadcast_to(avals[...].reshape(1, 2 * CC), (128, 2 * CC)).T
    ab[...] = loc_ab
    remote(gb_all(me4), gb_all(me4), gb_s.at[4], gb_r.at[4], sibling).wait_recv()
    remote(gb_all(p_partner), gb_all(p_partner), gb_s.at[5], gb_r.at[5], sibling).wait_recv()
    project(0, 0)
    gather(0, 2)
    project(0, 1)
    project(0, 7)
    for half in (0, 1):
        srcs = ring_last(half, brecv, b_s, b_r, part_sizes) + list(b_own(z, half))
        add_rows(PART, store(eg.at[1, z, pl.ds(half * PART, PART)]), srcs)
    gather(1, 0)
    gather(0, 3)
    project(0, 2)
    project(0, 6)
    project(1, 0)
    for i in range(NZ):
        for h in range(2):
            to = i * OB + h * HALF
            at = h * (OUT_WIN // 2) + i * HALF
            g4p[:, to : to + HALF] = g4[:, at : at + HALF]
    gather(1, 1)
    for n in range(3):
        remote(gvs, gv.at[me4], gv_s.at[n], gv_r.at[n], others[n]).wait_recv()
    gv[me4] = gvs[...]
    gather_last(0)
    kl_a = scale(0)
    back_chunks(0, (4,))
    back_step(0, 0, 0)
    back_chunks(0, (3, 5))
    back_step(0, 1, 1)
    gather(1, 2)
    project(1, 1)
    project(1, 7)
    back_chunks(0, (2, 6))
    gram_own()
    gather(1, 3)
    project(1, 2)
    project(1, 6)
    back_step(0, 1, 0)
    back_step(0, 2, 1)
    gather_last(1)
    kl_b = scale(1)
    klbuf[0] = jnp.full((8, 128), jnp.sum(kl_a + kl_b), F32)
    kl_z = kl_round(
        0, NZ, lambda k: (z + k) % NZ, lambda k: dev(z_=(z + k) % NZ), klz, klz_s, klz_r
    )
    back_chunks(1, (4,))
    back_step(1, 0, 0)
    back_chunks(1, (3, 5))
    back_step(1, 1, 1)
    gram_step(0, 0)
    gram_step(1, 1)
    back_chunks(0, (1, 7, 0))
    back_step(0, 2, 0)
    back_step(0, 3, 1)
    back_chunks(1, (2, 6))
    kl_z()
    kl_y = kl_round(
        1, 4, lambda k: (y + k) % 4, lambda k: dev(y_=(y + k) % 4), kly, kly_s, kly_r
    )
    back_step(1, 1, 0)
    back_step(1, 2, 1)
    gram_step(1, 0)
    back_step(0, 3, 0)
    gram_step(2, 1)
    back_chunks(1, (1, 7, 0))
    kl_y()
    kl_x = kl_round(
        2, 4,
        lambda k: (xh ^ (k // 2)) * 2 + (xl ^ (k % 2)),
        lambda k: dev(xh_=xh ^ (k // 2), xl_=xl ^ (k % 2)),
        klx, klx_s, klx_r,
    )
    back_step(1, 2, 0)
    back_step(1, 3, 1)
    gram_step(2, 0)
    final_send(0)
    back_step(1, 3, 0)
    gram_step(3, 1)
    kl_x()
    kl_c = kl_round(
        3, 2, lambda k: core if k == 0 else 1 - core, lambda k: sibling, klc, klc_s, klc_r
    )
    gram_step(3, 0)
    drain()
    final_send(1)
    out_a = final_dot(0)
    total[...] = out_a
    for half in (0, 1):
        srcs = ring_last(half, grecv, gz_s, gz_r, gram_sizes)
        srcs.append(load(gown.at[z], half * GL))
        size = gram_sizes[half]
        add_rows(size, store(gram.at[pl.ds(half * GL, size)]), srcs)
    kl_c()
    gain[...] = jnp.sqrt(OUT_WIN * FEAT / klbuf[4])
    total[...] = total[...] + final_dot(1)
    drain()


def finish(total, gram, gain, afac, gfac, update, new_a, new_g):
    update[...] = total[...] * gain[0:1, 0:1]
    fresh = (1.0 - DECAY) / TOKENS
    new_g[...] = DECAY * gfac[...] + fresh * gram[0:GW, :]
    new_a[:, 0:384] = DECAY * afac[:, 0:384] + fresh * gram[GW : GW + AW, :]
    new_a[:, 384:768] = DECAY * afac[:, 384:768] + fresh * gram[GW + AW : GR, :]


def per_device(
    activations, out_grads, a_basis, a_values, g_basis, g_values, owners, a_factors, g_factors
):
    workers = jnp.arange(owners.shape[1], dtype=jnp.int32)
    inverse = jnp.sum(
        jnp.where(owners[:, None, :] == workers[None, :, None], workers[None, None, :], 0), axis=2
    )
    vmem = pl.BlockSpec(memory_space=pltpu.VMEM)
    smem = pl.BlockSpec(memory_space=pltpu.SMEM)
    hbm = pl.BlockSpec(memory_space=pl.ANY)
    sem = pltpu.SemaphoreType.DMA
    v = pltpu.VMEM
    ring_a = (2, 2, 4, CH, OB)
    ring_b = (2, 2, 4, CH // 2, OB)
    scratch = [
        v((512, 768), BF16), v((512, OUT_WIN), BF16), v((768, 768), BF16),
        v((768, 768), BF16), v((768, 512), BF16), v((NZ, CC, OB), F32),
        v((NZ, CC, OB), BF16), v((NZ, CC, OB), BF16),
        v(ring_a, BF16), v(ring_a, BF16),
        v((CH, OB), BF16), v((CH, OB), BF16), v((CH, OB), F32),
        v((NZ, CH, OB), BF16), v((NZ, CH, OB), BF16), v(ring_b, BF16), v(ring_b, BF16),
        v((2, NZ, CH, OB), BF16), v((4 * GW, OUT_WIN), BF16), v((4 * GW, OUT_WIN), BF16),
        v((4, 8, GW), F32), v((8, GW), F32),
        v((768, 128), F32), v((2, CH, OB), F32), v((2, CH, OB), BF16),
        v((2, NZ, CH, OB), F32), v((2, *ring_b), BF16), v((2, *ring_b), BF16),
        v((2, 4, GW, CH), BF16), v((2, 4, GW, CH), BF16),
        v((32, GW, OB), F32), v((32, AW, 768), F32),
        v((2, NZ, GR, OB), BF16), v((2, NZ, GR, OB), BF16),
        v((NZ, GR, OB), BF16), v((NZ, GR, OB), BF16), v((NZ, GR, OB), F32),
        v((2, 2, 4, GL, OB), BF16), v((2, 2, 4, GL, OB), BF16),
        v((5, 8, 128), F32), v((NZ, 8, 128), F32), v((4, 8, 128), F32), v((4, 8, 128), F32),
        v((2, 8, 128), F32),
        sem((NZ,)), sem((NZ,)), sem((2, 2, 4)), sem((2, 2, 4)), sem((1,)), sem((1,)),
        sem((NZ,)), sem((NZ,)), sem((2, 2, 4)), sem((2, 2, 4)),
        sem((2, 2, 2, 4)), sem((2, 2, 2, 4)), sem((2, 2, 2, 4)), sem((2, 2, 2, 4)),
        sem((2, 3)), sem((2, 3)),
        sem((2,)), sem((2,)), sem((1,)), sem((1,)), sem((2, 2, 4)), sem((2, 2, 4)),
        sem((6,)), sem((6,)), sem((3,)), sem((3,)),
        sem((NZ,)), sem((NZ,)), sem((4,)), sem((4,)), sem((4,)), sem((4,)), sem((2,)), sem((2,)),
        sem((6,)),
    ]
    total, gram, gain = pl.pallas_call(
        kernel,
        out_shape=(
            jax.ShapeDtypeStruct((GW, 768), F32),
            jax.ShapeDtypeStruct((GR, OB), F32),
            jax.ShapeDtypeStruct((8, 128), F32),
        ),
        in_specs=[hbm] * 4 + [vmem] * 2 + [smem],
        out_specs=(vmem, vmem, vmem),
        scratch_shapes=scratch,
        compiler_params=pltpu.CompilerParams(
            collective_id=0, has_side_effects=True, vmem_limit_bytes=60 << 20
        ),
        cost_estimate=pl.CostEstimate(
            flops=5_400_000_000, bytes_accessed=8_000_000, transcendentals=0
        ),
        name="precondition",
    )(activations, out_grads, a_basis, g_basis.T, a_values, g_values, inverse)
    return pl.pallas_call(
        finish,
        out_shape=(
            jax.ShapeDtypeStruct((GW, 768), F32),
            jax.ShapeDtypeStruct((AW, 768), F32),
            jax.ShapeDtypeStruct((GW, OB), F32),
        ),
        in_specs=[vmem] * 5,
        out_specs=(vmem, vmem, vmem),
        name="finish",
    )(total, gram, gain, a_factors, g_factors)


def solution(mesh):
    in_specs = (
        P("dp", "tensor"),
        P("dp", None),
        P("tensor", None),
        P("tensor"),
        P(None, "dp"),
        P("dp"),
        P(),
        P("dp", "tensor"),
        P("dp", "tensor"),
    )
    out_specs = (P("dp", "tensor"), P("dp", "tensor"), P("dp", "tensor"))
    return jax.shard_map(
        per_device, mesh=mesh, in_specs=in_specs, out_specs=out_specs, check_vma=False
    )
```

```python
import functools

import jax
import jax.numpy as jnp
from jax import lax
from jax.experimental import pallas as pl
from jax.experimental.pallas import tpu as pltpu
from jax.sharding import PartitionSpec as P

FEAT = 6144
OUT_WIN = 3072
TOKENS = 16384
DECAY = 0.5
DAMPING = 0.1
F32 = jnp.float32
BF16 = jnp.bfloat16
MESH = pl.DeviceIdType.MESH

NZ = 8
CC = 384
HALF = 192
CH = 96
OB = 384
GW = 96
AW = 24
GR = 144
GL = 80

NT = (((1,), (1,)), ((), ()))
TN = (((0,), (0,)), ((), ()))


def dot(a, b, dims=(((1,), (0,)), ((), ()))):
    return lax.dot_general(a, b, dims, preferred_element_type=F32)


def add_rows(rows, dst, srcs, step=16):
    def body(i, _):
        at = pl.ds(pl.multiple_of(i * step, step), step)
        total = srcs[0](at).astype(F32)
        for src in srcs[1:]:
            total = total + src(at).astype(F32)
        dst(at, total)
        return 0

    lax.fori_loop(0, rows // step, body, 0, unroll=2)


def store(ref):
    def put(at, value):
        ref[at, :] = value.astype(ref.dtype)

    return put


def load(ref, first=0):
    def get(at):
        return ref[pl.ds(first + at.start, at.size), :]

    return get


def kernel(
    acts_in, grads_in, qa_in, gbasis_in, avals, gvals, owners,
    total, gram, gain,
    acts, grads, qa, qat, apt, own, csend, crecv,
    asend, arecv, xsend, xrecv, xown, xbs, xbr, bsend, brecv,
    eg, g4, g4p, gv, gvs, ab, proj, scl,
    rown, rsend, rrecv, fsend, frecv,
    gramg, grama, gcs, gcr, gxs, gxr, gown, gsend, grecv,
    klbuf, klz, kly, klx, klc, inv_rows, inv,
    c_s, c_r, a_s, a_r, x_s, x_r, xb_s, xb_r, b_s, b_r, e_s, e_r, r_s, r_r, f_s, f_r,
    gc_s, gc_r, gx_s, gx_r, gz_s, gz_r, gb_s, gb_r, gv_s, gv_r,
    klz_s, klz_r, kly_s, kly_r, klx_s, klx_r, klc_s, klc_r, loc,
):
    dp = lax.axis_index("dp")
    tensor = lax.axis_index("tensor")
    core = dp % 2
    z = (dp // 2) % NZ
    xh = dp // (2 * NZ)
    y = tensor // 2
    xl = tensor % 2

    def dev(xh_=xh, z_=z, core_=core, y_=y, xl_=xl):
        return ((xh_ * NZ + z_) * 2 + core_, y_ * 2 + xl_)

    sibling = dev(core_=1 - core)
    partner = dev(xh_=1 - xh)
    partner_sibling = dev(xh_=1 - xh, core_=1 - core)
    ring = (dev(z_=(z + 1) % NZ), dev(z_=(z + NZ - 1) % NZ))
    pending = []

    def remote(src, dst, ss, rs, to):
        return pltpu.make_async_remote_copy(
            src_ref=src, dst_ref=dst, send_sem=ss, recv_sem=rs, device_id=to, device_id_type=MESH
        )

    def send(*args):
        copy = remote(*args)
        copy.start()
        pending.append(copy)
        return copy

    def drain(keep=0):
        old = pending[: len(pending) - keep]
        for copy in old:
            copy.wait_send()
        del pending[: len(old)]

    barrier = pltpu.get_barrier_semaphore()

    def greet(to):
        pl.semaphore_signal(barrier, inc=1, device_id=to, device_id_type=MESH)

    me4 = xh * 2 + core
    mine4 = pl.ds(pl.multiple_of(me4 * GW, GW), GW)
    loads = [
        pltpu.make_async_copy(qa_in, qa, loc.at[0]),
        pltpu.make_async_copy(acts_in, acts, loc.at[1]),
        pltpu.make_async_copy(grads_in, grads, loc.at[2]),
        pltpu.make_async_copy(gbasis_in, g4.at[mine4], loc.at[3]),
    ]
    for copy in loads:
        copy.start()
    greet(sibling)
    greet(partner)
    greet(partner_sibling)
    for k in range(1, NZ):
        greet(dev(z_=(z + k) % NZ))
    for k in range(1, 4):
        greet(dev(y_=(y + k) % 4))
    greet(dev(xl_=1 - xl))
    greet(dev(xh_=1 - xh, xl_=1 - xl))

    for i in range(2):
        worker = lax.broadcasted_iota(jnp.int32, (32, 32), 0)
        block = lax.broadcasted_iota(jnp.int32, (32, 32), 1)
        here = jnp.where(jnp.broadcast_to(owners[i : i + 1, :], (32, 32)) == worker, block, 0)
        inv_rows[i] = jnp.broadcast_to(jnp.max(here, axis=1, keepdims=True), (32, 128))
    inv_copy = pltpu.make_async_copy(inv_rows, inv, loc.at[6])
    inv_copy.start()

    loads[0].wait()
    for i in range(6):
        qat[128 * i : 128 * (i + 1), :] = qa[:, 128 * i : 128 * (i + 1)].T
    loads[1].wait()
    for i in range(2):
        apt[384 * i : 384 * (i + 1), :] = dot(
            qat[384 * i : 384 * (i + 1), :], acts[...], NT
        ).astype(BF16)
    loads[2].wait()

    def chunk(k):
        d = (z + k) % NZ
        block = grads[:, pl.ds(pl.multiple_of(d * OB, 128), OB)]
        theirs = pl.ds(pl.multiple_of((1 - core) * CC, CC), CC)
        csend[d] = dot(apt[theirs, :], block).astype(BF16)
        return d, block

    def chunk_send(d):
        return remote(csend.at[d], crecv.at[d], c_s.at[d], c_r.at[d], sibling)

    def chunk_own(d, block):
        mine = pl.ds(pl.multiple_of(core * CC, CC), CC)
        own[d] = dot(apt[mine, :], block)

    d0, block0 = chunk(4)
    loads[3].wait()
    gvs[...] = jnp.broadcast_to(gvals[...].reshape(1, GW), gvs.shape)
    pl.semaphore_wait(barrier, 15)
    pending.append(chunk_send(d0))
    pending[-1].start()

    quarter = OUT_WIN // 4

    def gb_part(p, y_):
        rows = pl.ds(pl.multiple_of(p * GW, GW), GW)
        return g4.at[rows, pl.ds(pl.multiple_of(y_ * quarter, 128), quarter)]

    def gb_all(p):
        return g4.at[pl.ds(pl.multiple_of(p * GW, GW), GW)]

    p_partner = (1 - xh) * 2 + core
    send(gb_part(me4, y), gb_part(me4, y), gb_s.at[0], gb_r.at[y], partner)
    chunk_own(d0, block0)

    def offset(direction, it):
        k = 4 - it
        return k if direction == 0 else (NZ - k) % NZ

    def ring_step(it, parity, own_half, sbuf, rbuf, ss, rs, sizes):
        for direction in range(2):
            half = parity if direction == 0 else 1 - parity
            size = sizes[half]
            d = (z + offset(direction, it)) % NZ
            srcs = list(own_half(d, half))
            rows = pl.ds(0, size)
            if it > parity:
                before = rbuf.at[direction, half, it - 1, rows]
                remote(
                    before, before, ss.at[direction, half, it - 1],
                    rs.at[direction, half, it - 1], ring[direction],
                ).wait_recv()
                srcs.append(load(rbuf.at[direction, half, it - 1]))
            add_rows(size, store(sbuf.at[direction, half, it]), srcs)
            send(
                sbuf.at[direction, half, it, rows], rbuf.at[direction, half, it, rows],
                ss.at[direction, half, it], rs.at[direction, half, it], ring[direction],
            )

    def ring_last(half, rbuf, ss, rs, sizes):
        rows = pl.ds(0, sizes[half])
        for direction in range(2):
            last = rbuf.at[direction, half, 3, rows]
            remote(
                last, last, ss.at[direction, half, 3], rs.at[direction, half, 3], ring[direction]
            ).wait_recv()
        return [load(rbuf.at[0, half, 3]), load(rbuf.at[1, half, 3])]

    a_sizes = (CH, CH)
    part_sizes = (CH // 2, CH // 2)
    gram_sizes = (GL, GR - GL)
    PART = CH // 2

    def chunks(ks):
        for k in ks:
            d, block = chunk(k)
            pending.append(chunk_send(d))
            pending[-1].start()
            chunk_own(d, block)

    def chunks_wait(ks):
        for k in ks:
            chunk_send((z + k) % NZ).wait_recv()

    def a_own(d, half):
        return load(own.at[d], half * CH), load(crecv.at[d], half * CH)

    def a_step(it, parity):
        ring_step(it, parity, a_own, asend, arecv, a_s, a_r, a_sizes)

    def bx_copy(d):
        return remote(xbs.at[d], xbr.at[d], xb_s.at[d], xb_r.at[d], partner)

    def bx_send(ks):
        for k in ks:
            d = (z + k) % NZ
            at = HALF + (1 - xh) * CH
            add_rows(CH, store(xbs.at[d]), [load(own.at[d], at), load(crecv.at[d], at)])
            copy = bx_copy(d)
            copy.start()
            pending.append(copy)

    def bx_wait(ks):
        for k in ks:
            bx_copy((z + k) % NZ).wait_recv()

    def b_own(d, half):
        at = HALF + xh * CH + half * PART
        return load(own.at[d], at), load(crecv.at[d], at), load(xbr.at[d], half * PART)

    def b_step(it, parity):
        ring_step(it, parity, b_own, bsend, brecv, b_s, b_r, part_sizes)

    def gram_g(first, last):
        mine = grads[:, pl.ds(pl.multiple_of(tensor * OB, 128), OB)]

        def body(i, _):
            at = pl.multiple_of(i * 384, 128)
            part = dot(grads[:, pl.ds(at, 384)], mine, TN)
            gramg[pl.ds(i * 4, 4)] = part.reshape(4, GW, OB)
            return 0

        lax.fori_loop(first, last, body, 0)

    def gram_a():
        def body(i, _):
            at = pl.multiple_of(i * 384, 128)
            part = dot(acts[:, pl.ds(at, 384)], acts[...], TN)
            grama[pl.ds(i * 16, 16)] = part.reshape(16, AW, 2 * CC)
            return 0

        lax.fori_loop(0, 2, body, 0)

    def gram_block(xh_, z_, core_):
        w = (xh_ * NZ + z_) * 2 + core_
        return gramg[inv[1, w, 0]], grama[inv[0, w, 0]]

    def put_block(ref, g_part, a_part):
        ref[0:GW, :] = g_part.astype(ref.dtype)
        tail = jnp.concatenate([a_part[:, 0:384], a_part[:, 384:768]], axis=0)
        ref[GW:GR, :] = tail.astype(ref.dtype)

    def gram_core(turn):
        other = 1 - xh if turn == 0 else xh

        def body(i, _):
            put_block(gcs.at[turn, i], *gram_block(other, i, 1 - core))
            return 0

        lax.fori_loop(0, NZ, body, 0)
        send(gcs.at[turn], gcr.at[turn], gc_s.at[turn], gc_r.at[turn], sibling)

    def gram_add(d, dst, xh_, others):
        put_block(gown.at[d], *gram_block(xh_, d, core))
        add_rows(GR, store(dst), [load(gown.at[d])] + [load(other) for other in others])

    def gx_copy(d):
        return remote(gxs.at[d], gxr.at[d], gx_s.at[d], gx_r.at[d], partner)

    def gram_wait(turn):
        remote(gcs.at[turn], gcr.at[turn], gc_s.at[turn], gc_r.at[turn], sibling).wait_recv()

    def gram_x(ks):
        for k in ks:
            d = (z + k) % NZ
            gram_add(d, gxs.at[d], 1 - xh, [gcr.at[0, d]])
            copy = gx_copy(d)
            copy.start()
            pending.append(copy)

    def gram_own(ks):
        for k in ks:
            d = (z + k) % NZ
            gx_copy(d).wait_recv()
            gram_add(d, gown.at[d], xh, [gcr.at[1, d], gxr.at[d]])

    def gram_half(d, half):
        return (load(gown.at[d], half * GL),)

    def gram_step(it, parity):
        ring_step(it, parity, gram_half, gsend, grecv, gz_s, gz_r, gram_sizes)

    def gather_copy(s, direction, half, it):
        b = (z + NZ - it) % NZ if direction == 0 else (z + it) % NZ
        part = eg.at[s, b, pl.ds(half * PART, PART)]
        return remote(
            part, part, e_s.at[s, direction, half, it], e_r.at[s, direction, half, it],
            ring[direction],
        )

    def gather(s, it):
        for half in (0, 1):
            for direction in (0, 1):
                side = half if direction == 0 else 1 - half
                if half == 1 and it == 3:
                    continue
                if it > 0:
                    gather_copy(s, direction, side, it - 1).wait_recv()
                copy = gather_copy(s, direction, side, it)
                copy.start()
                pending.append(copy)

    def gather_last(s):
        gather_copy(s, 0, 1, 2).wait_recv()
        gather_copy(s, 1, 0, 2).wait_recv()
        project(s, 3)
        project(s, 5)
        gather_copy(s, 0, 0, 3).wait_recv()
        gather_copy(s, 1, 1, 3).wait_recv()
        project(s, 4)

    def project(s, k):
        b = (z + k) % NZ
        part = dot(eg[s, b], g4[:, pl.ds(pl.multiple_of(b * OB, 128), OB)], NT)
        proj[s] = part if k == 0 else proj[s] + part

    def scale(s):
        g_row = jnp.concatenate([gv[p, 0:1, :] for p in range(4)], axis=1)
        first = core * CC + s * HALF + xh * CH

        def body(i, kl):
            at = pl.multiple_of(i * 16, 16)
            value = proj[s, pl.ds(at, 16), :]
            a_col = ab[pl.ds(pl.multiple_of(first + at, 16), 16), 0:1]
            scaled = value / (a_col * g_row + DAMPING)
            scl[s, pl.ds(at, 16), :] = scaled.astype(BF16)
            return kl + value * scaled

        return lax.fori_loop(0, CH // 16, body, jnp.zeros((16, OB), F32))

    def back_chunks(s, ks):
        for k in ks:
            d = (z + k) % NZ
            rown[s, d] = dot(scl[s], g4p[:, pl.ds(pl.multiple_of(d * OB, 128), OB)])

    def back_step(s, it, parity):
        def back_own(d, half):
            return (load(rown.at[s, d], half * PART),)

        ring_step(
            it, parity, back_own, rsend.at[s], rrecv.at[s], r_s.at[s], r_r.at[s], part_sizes
        )

    places = (
        (sibling, xh * 2 + 1 - core, (1 - core) * 2 + xh),
        (partner, (1 - xh) * 2 + core, core * 2 + 1 - xh),
        (partner_sibling, (1 - xh) * 2 + 1 - core, (1 - core) * 2 + 1 - xh),
    )
    j = core * 2 + xh

    def final_copy(s, n):
        to, p, _ = places[n]
        return remote(fsend.at[s, p], frecv.at[s, j], f_s.at[s, n], f_r.at[s, n], to)

    def final_keep(s):
        return pltpu.make_async_copy(fsend.at[s, me4], frecv.at[s, j], loc.at[4 + s])

    def final_send(s):
        for half in (0, 1):
            srcs = ring_last(half, rrecv.at[s], r_s.at[s], r_r.at[s], part_sizes)
            srcs.append(load(rown.at[s, z], half * PART))
            add_rows(PART, store(xown.at[pl.ds(half * PART, PART)]), srcs)
        turned = xown[...].T.astype(BF16)
        for p in range(4):
            fsend[s, p] = turned[p * GW : (p + 1) * GW, :]
        for n in (1, 2, 0):
            copy = final_copy(s, n)
            copy.start()
            pending.append(copy)
        final_keep(s).start()

    def final_dot(s):
        final_keep(s).wait()
        for n in (0, 1, 2):
            to, p, slot = places[n]
            remote(
                fsend.at[s, p], frecv.at[s, slot], f_s.at[s, n], f_r.at[s, n], to
            ).wait_recv()
        out = None
        for i in range(4):
            first = (i // 2) * CC + s * HALF + (i % 2) * CH
            part = dot(frecv[s, i], qat[first : first + CH, :])
            out = part if out is None else out + part
        return out

    def kl_round(stage, count, place, peer, buf, ss, rs):
        copies = []
        for k in range(1, count):
            send(klbuf.at[stage], buf.at[place(0)], ss.at[k], rs.at[place(0)], peer(k))
            copies.append(
                remote(klbuf.at[stage], buf.at[place(k)], ss.at[k], rs.at[place(k)], peer(k))
            )

        def finish():
            value = klbuf[stage]
            for k in range(1, count):
                copies[k - 1].wait_recv()
                value = value + buf[place(k)]
            klbuf[stage + 1] = value

        return finish

    def gb_forward():
        part = gb_part(p_partner, y)
        remote(part, part, gb_s.at[0], gb_r.at[y], partner).wait_recv()
        for k in range(1, 4):
            send(part, part, gb_s.at[k], gb_r.at[y], dev(y_=(y + k) % 4))
        send(gb_all(me4), gb_all(me4), gb_s.at[4], gb_r.at[4], sibling)

    def gb_sibling():
        for k in range(1, 4):
            y_ = (y + k) % 4
            there = gb_part(p_partner, y_)
            remote(there, there, gb_s.at[k], gb_r.at[y_], dev(y_=y_)).wait_recv()
        send(gb_all(p_partner), gb_all(p_partner), gb_s.at[5], gb_r.at[5], sibling)

    def gb_wait():
        for n, p in ((4, me4), (5, p_partner)):
            remote(gb_all(p), gb_all(p), gb_s.at[n], gb_r.at[n], sibling).wait_recv()

    others = (sibling, partner, partner_sibling)

    def gv_copy(n):
        return remote(gvs, gv.at[me4], gv_s.at[n], gv_r.at[n], others[n])

    def turn_columns():
        for i in range(NZ):
            for h in range(2):
                to = i * OB + h * HALF
                at = h * (OUT_WIN // 2) + i * HALF
                g4p[:, to : to + HALF] = g4[:, at : at + HALF]

    def a_last():
        for half in (0, 1):
            ring_last(half, arecv, a_s, a_r, a_sizes)

        def srcs(half):
            at = pl.multiple_of(half * CH, CH)
            return [
                load(own.at[z], at), load(crecv.at[z], at),
                load(arecv.at[0, half, 3]), load(arecv.at[1, half, 3]),
            ]

        add_rows(CH, store(xsend), srcs(1 - xh))
        send(xsend, xrecv, x_s.at[0], x_r.at[0], partner)
        add_rows(CH, store(xown), srcs(xh))

    def a_done():
        remote(xsend, xrecv, x_s.at[0], x_r.at[0], partner).wait_recv()
        add_rows(CH, store(eg.at[0, z]), [load(xown), load(xrecv)])

    def b_done():
        for half in (0, 1):
            srcs = ring_last(half, brecv, b_s, b_r, part_sizes) + list(b_own(z, half))
            add_rows(PART, store(eg.at[1, z, pl.ds(half * PART, PART)]), srcs)

    chunks((3, 5))
    chunks_wait((4,))
    a_step(0, 0)
    bx_send((4,))
    chunks_wait((3, 5))
    a_step(1, 1)
    bx_send((3, 5))
    chunks((2, 6))
    gram_g(0, 2)
    a_step(1, 0)
    chunks_wait((2, 6))
    bx_send((2, 6))
    chunks((1, 7, 0))
    a_step(2, 1)
    bx_wait((4,))
    b_step(0, 0)
    chunks_wait((1, 7, 0))
    bx_send((1, 7, 0))
    gram_g(2, 3)
    a_step(2, 0)
    gb_forward()
    for n in range(3):
        copy = gv_copy(n)
        copy.start()
        pending.append(copy)
    bx_wait((3, 5))
    b_step(1, 1)
    gram_g(3, 4)
    a_step(3, 1)
    b_step(1, 0)
    gram_g(4, 6)
    a_step(3, 0)
    bx_wait((2, 6))
    b_step(2, 1)
    gram_g(6, 8)
    b_step(2, 0)
    gram_a()
    a_last()
    inv_copy.wait()
    gram_core(0)
    bx_wait((1, 7))
    b_step(3, 1)
    gram_core(1)
    b_step(3, 0)
    gram_wait(0)
    gram_x((4, 3, 5))
    a_done()
    gather(0, 0)
    bx_wait((0,))
    b_done()
    gather(1, 0)
    gram_x((2, 6, 1, 7, 0))
    gram_wait(1)
    gb_sibling()
    ab[...] = jnp.broadcast_to(avals[...].reshape(1, 2 * CC), (128, 2 * CC)).T
    gather(0, 1)
    gram_own((4,))
    gram_step(0, 0)
    gather(1, 1)
    gb_wait()
    project(0, 0)
    project(1, 0)
    gram_own((3, 5))
    gram_step(1, 1)
    for k in (1, 7):
        project(0, k)
    gather(0, 2)
    for k in (1, 7):
        project(1, k)
    gather(1, 2)
    gram_step(1, 0)
    turn_columns()
    for n in range(3):
        gv_copy(n).wait_recv()
    gv[me4] = gvs[...]
    for k in (2, 6):
        project(0, k)
    gather(0, 3)
    gram_own((2, 6))
    gram_step(2, 1)
    for k in (2, 6):
        project(1, k)
    gather(1, 3)
    gather_last(0)
    kl_a = scale(0)
    back_chunks(0, (4,))
    back_step(0, 0, 0)
    back_chunks(0, (3, 5))
    back_step(0, 1, 1)
    gather_last(1)
    kl_b = scale(1)
    klbuf[0] = jnp.full((8, 128), jnp.sum(kl_a + kl_b), F32)
    kl_z = kl_round(
        0, NZ, lambda k: (z + k) % NZ, lambda k: dev(z_=(z + k) % NZ), klz, klz_s, klz_r
    )
    back_chunks(1, (4,))
    back_step(1, 0, 0)
    back_chunks(1, (3, 5))
    back_step(1, 1, 1)
    back_chunks(0, (2, 6))
    back_step(0, 1, 0)
    back_step(0, 2, 1)
    back_chunks(1, (2, 6))
    back_step(1, 1, 0)
    back_step(1, 2, 1)
    gram_step(2, 0)
    gram_own((1, 7, 0))
    kl_z()
    kl_y = kl_round(
        1, 4, lambda k: (y + k) % 4, lambda k: dev(y_=(y + k) % 4), kly, kly_s, kly_r
    )
    back_chunks(0, (1, 7, 0))
    back_step(0, 2, 0)
    back_step(0, 3, 1)
    back_chunks(1, (1, 7, 0))
    back_step(1, 2, 0)
    back_step(1, 3, 1)
    gram_step(3, 1)
    kl_y()
    kl_x = kl_round(
        2, 4,
        lambda k: (xh ^ (k // 2)) * 2 + (xl ^ (k % 2)),
        lambda k: dev(xh_=xh ^ (k // 2), xl_=xl ^ (k % 2)),
        klx, klx_s, klx_r,
    )
    drain(24)
    back_step(0, 3, 0)
    back_step(1, 3, 0)
    gram_step(3, 0)
    kl_x()
    kl_c = kl_round(
        3, 2, lambda k: core if k == 0 else 1 - core, lambda k: sibling, klc, klc_s, klc_r
    )
    final_send(0)
    final_send(1)
    out_a = final_dot(0)
    total[...] = out_a
    kl_c()
    gain[...] = jnp.sqrt(OUT_WIN * FEAT / klbuf[4])
    drain(12)
    for half in (0, 1):
        srcs = ring_last(half, grecv, gz_s, gz_r, gram_sizes)
        srcs.append(load(gown.at[z], half * GL))
        size = gram_sizes[half]
        add_rows(size, store(gram.at[pl.ds(half * GL, size)]), srcs)
    total[...] = total[...] + final_dot(1)
    drain()


def finish(total, gram, gain, afac, gfac, update, new_a, new_g):
    update[...] = total[...] * gain[0:1, 0:1]
    fresh = (1.0 - DECAY) / TOKENS
    new_g[...] = DECAY * gfac[...] + fresh * gram[0:GW, :]
    new_a[:, 0:384] = DECAY * afac[:, 0:384] + fresh * gram[GW : GW + AW, :]
    new_a[:, 384:768] = DECAY * afac[:, 384:768] + fresh * gram[GW + AW : GR, :]


def per_device(
    activations, out_grads, a_basis, a_values, g_basis, g_values, owners, a_factors, g_factors
):
    vmem = pl.BlockSpec(memory_space=pltpu.VMEM)
    hbm = pl.BlockSpec(memory_space=pl.ANY)
    sem = pltpu.SemaphoreType.DMA
    v = pltpu.VMEM
    ring_a = (2, 2, 4, CH, OB)
    ring_b = (2, 2, 4, CH // 2, OB)
    scratch = [
        v((512, 768), BF16), v((512, OUT_WIN), BF16), v((768, 768), BF16),
        v((768, 768), BF16), v((768, 512), BF16), v((NZ, CC, OB), F32),
        v((NZ, CC, OB), BF16), v((NZ, CC, OB), BF16),
        v(ring_a, BF16), v(ring_a, BF16),
        v((CH, OB), BF16), v((CH, OB), BF16), v((CH, OB), F32),
        v((NZ, CH, OB), BF16), v((NZ, CH, OB), BF16), v(ring_b, BF16), v(ring_b, BF16),
        v((2, NZ, CH, OB), BF16), v((4 * GW, OUT_WIN), BF16), v((4 * GW, OUT_WIN), BF16),
        v((4, 8, GW), F32), v((8, GW), F32),
        v((768, 128), F32), v((2, CH, OB), F32), v((2, CH, OB), BF16),
        v((2, NZ, CH, OB), F32), v((2, *ring_b), BF16), v((2, *ring_b), BF16),
        v((2, 4, GW, CH), BF16), v((2, 4, GW, CH), BF16),
        v((32, GW, OB), F32), v((32, AW, 768), F32),
        v((2, NZ, GR, OB), BF16), v((2, NZ, GR, OB), BF16),
        v((NZ, GR, OB), BF16), v((NZ, GR, OB), BF16), v((NZ, GR, OB), F32),
        v((2, 2, 4, GL, OB), BF16), v((2, 2, 4, GL, OB), BF16),
        v((5, 8, 128), F32), v((NZ, 8, 128), F32), v((4, 8, 128), F32), v((4, 8, 128), F32),
        v((2, 8, 128), F32), v((2, 32, 128), jnp.int32), pltpu.SMEM((2, 32, 128), jnp.int32),
        sem((NZ,)), sem((NZ,)), sem((2, 2, 4)), sem((2, 2, 4)), sem((1,)), sem((1,)),
        sem((NZ,)), sem((NZ,)), sem((2, 2, 4)), sem((2, 2, 4)),
        sem((2, 2, 2, 4)), sem((2, 2, 2, 4)), sem((2, 2, 2, 4)), sem((2, 2, 2, 4)),
        sem((2, 3)), sem((2, 3)),
        sem((2,)), sem((2,)), sem((NZ,)), sem((NZ,)), sem((2, 2, 4)), sem((2, 2, 4)),
        sem((6,)), sem((6,)), sem((3,)), sem((3,)),
        sem((NZ,)), sem((NZ,)), sem((4,)), sem((4,)), sem((4,)), sem((4,)), sem((2,)), sem((2,)),
        sem((7,)),
    ]
    total, gram, gain = pl.pallas_call(
        kernel,
        out_shape=(
            jax.ShapeDtypeStruct((GW, 768), F32),
            jax.ShapeDtypeStruct((GR, OB), F32),
            jax.ShapeDtypeStruct((8, 128), F32),
        ),
        in_specs=[hbm] * 4 + [vmem] * 3,
        out_specs=(vmem, vmem, vmem),
        scratch_shapes=scratch,
        compiler_params=pltpu.CompilerParams(
            collective_id=0, has_side_effects=True, vmem_limit_bytes=60 << 20
        ),
        cost_estimate=pl.CostEstimate(
            flops=5_400_000_000, bytes_accessed=8_000_000, transcendentals=0
        ),
        name="precondition",
    )(activations, out_grads, a_basis, g_basis.T, a_values, g_values, owners)
    return pl.pallas_call(
        finish,
        out_shape=(
            jax.ShapeDtypeStruct((GW, 768), F32),
            jax.ShapeDtypeStruct((AW, 768), F32),
            jax.ShapeDtypeStruct((GW, OB), F32),
        ),
        in_specs=[vmem] * 5,
        out_specs=(vmem, vmem, vmem),
        name="finish",
    )(total, gram, gain, a_factors, g_factors)


def solution(mesh):
    in_specs = (
        P("dp", "tensor"),
        P("dp", None),
        P("tensor", None),
        P("tensor"),
        P(None, "dp"),
        P("dp"),
        P(),
        P("dp", "tensor"),
        P("dp", "tensor"),
    )
    out_specs = (P("dp", "tensor"), P("dp", "tensor"), P("dp", "tensor"))
    return jax.shard_map(
        per_device, mesh=mesh, in_specs=in_specs, out_specs=out_specs, check_vma=False
    )
```

```python
import functools

import jax
import jax.numpy as jnp
from jax import lax
from jax.experimental import pallas as pl
from jax.experimental.pallas import tpu as pltpu
from jax.sharding import PartitionSpec as P

FEAT = 6144
OUT_WIN = 3072
TOKENS = 16384
DECAY = 0.5
DAMPING = 0.1
F32 = jnp.float32
BF16 = jnp.bfloat16
MESH = pl.DeviceIdType.MESH

NZ = 8
CC = 384
HALF = 192
CH = 96
OB = 384
GW = 96
AW = 24
GR = 144
GL = 80

NT = (((1,), (1,)), ((), ()))
TN = (((0,), (0,)), ((), ()))


def dot(a, b, dims=(((1,), (0,)), ((), ()))):
    return lax.dot_general(a, b, dims, preferred_element_type=F32)


def add_rows(rows, dst, srcs):
    step = 48 if rows % 48 == 0 else 16

    def body(i, _):
        at = pl.ds(pl.multiple_of(i * step, step), step)
        total = srcs[0](at).astype(F32)
        for src in srcs[1:]:
            total = total + src(at).astype(F32)
        dst(at, total)
        return 0

    lax.fori_loop(0, rows // step, body, 0, unroll=rows // step)


def store(ref):
    def put(at, value):
        ref[at, :] = value.astype(ref.dtype)

    return put


def load(ref, first=0):
    def get(at):
        return ref[pl.ds(first + at.start, at.size), :]

    return get


def kernel(
    acts_in, grads_in, qa_in, gbasis_in, avals, gvals, owners,
    total, gram, gain,
    acts, grads, qa, qat, apt, own, csend, crecv,
    asend, arecv, xsend, xrecv, xown, xbs, xbr, bsend, brecv,
    eg, g4, g4p, gv, gvs, ab, proj, scl,
    rown, rsend, rrecv, fsend, frecv,
    gramg, grama, gcs, gcr, gxs, gxr, gown, gsend, grecv,
    klbuf, klz, kly, klx, klc, inv_rows, inv,
    c_s, c_r, a_s, a_r, x_s, x_r, xb_s, xb_r, b_s, b_r, e_s, e_r, r_s, r_r, f_s, f_r,
    gc_s, gc_r, gx_s, gx_r, gz_s, gz_r, gb_s, gb_r, gv_s, gv_r,
    klz_s, klz_r, kly_s, kly_r, klx_s, klx_r, klc_s, klc_r, loc,
):
    dp = lax.axis_index("dp")
    tensor = lax.axis_index("tensor")
    core = dp % 2
    z = (dp // 2) % NZ
    xh = dp // (2 * NZ)
    y = tensor // 2
    xl = tensor % 2

    def dev(xh_=xh, z_=z, core_=core, y_=y, xl_=xl):
        return ((xh_ * NZ + z_) * 2 + core_, y_ * 2 + xl_)

    sibling = dev(core_=1 - core)
    partner = dev(xh_=1 - xh)
    partner_sibling = dev(xh_=1 - xh, core_=1 - core)
    ring = (dev(z_=(z + 1) % NZ), dev(z_=(z + NZ - 1) % NZ))
    pending = []

    def remote(src, dst, ss, rs, to):
        return pltpu.make_async_remote_copy(
            src_ref=src, dst_ref=dst, send_sem=ss, recv_sem=rs, device_id=to, device_id_type=MESH
        )

    def send(*args):
        copy = remote(*args)
        copy.start()
        pending.append(copy)
        return copy

    def drain(keep=0):
        old = pending[: len(pending) - keep]
        for copy in old:
            copy.wait_send()
        del pending[: len(old)]

    barrier = pltpu.get_barrier_semaphore()

    def greet(to):
        pl.semaphore_signal(barrier, inc=1, device_id=to, device_id_type=MESH)

    me4 = xh * 2 + core
    mine4 = pl.ds(pl.multiple_of(me4 * GW, GW), GW)
    loads = [
        pltpu.make_async_copy(qa_in, qa, loc.at[0]),
        pltpu.make_async_copy(acts_in, acts, loc.at[1]),
        pltpu.make_async_copy(grads_in, grads, loc.at[2]),
        pltpu.make_async_copy(gbasis_in, g4.at[mine4], loc.at[3]),
    ]
    for copy in loads:
        copy.start()
    greet(sibling)
    greet(partner)
    greet(partner_sibling)
    greet(ring[0])
    greet(ring[1])
    for k in range(1, 4):
        greet(dev(y_=(y + k) % 4))
    greet(dev(xl_=1 - xl))
    greet(dev(xh_=1 - xh, xl_=1 - xl))

    for i in range(2):
        worker = lax.broadcasted_iota(jnp.int32, (32, 32), 0)
        block = lax.broadcasted_iota(jnp.int32, (32, 32), 1)
        here = jnp.where(jnp.broadcast_to(owners[i : i + 1, :], (32, 32)) == worker, block, 0)
        inv_rows[i] = jnp.broadcast_to(jnp.max(here, axis=1, keepdims=True), (32, 128))
    inv_copy = pltpu.make_async_copy(inv_rows, inv, loc.at[6])
    inv_copy.start()

    loads[0].wait()
    for i in range(6):
        qat[128 * i : 128 * (i + 1), :] = qa[:, 128 * i : 128 * (i + 1)].T
    loads[1].wait()
    for i in range(2):
        apt[384 * i : 384 * (i + 1), :] = dot(
            qat[384 * i : 384 * (i + 1), :], acts[...], NT
        ).astype(BF16)
    loads[2].wait()

    def chunk(k):
        d = (z + k) % NZ
        block = grads[:, pl.ds(pl.multiple_of(d * OB, 128), OB)]
        theirs = pl.ds(pl.multiple_of((1 - core) * CC, CC), CC)
        csend[d] = dot(apt[theirs, :], block).astype(BF16)
        return d, block

    def chunk_send(d):
        return remote(csend.at[d], crecv.at[d], c_s.at[d], c_r.at[d], sibling)

    def chunk_own(d, block):
        mine = pl.ds(pl.multiple_of(core * CC, CC), CC)
        own[d] = dot(apt[mine, :], block)

    d0, block0 = chunk(4)
    loads[3].wait()
    gvs[...] = jnp.broadcast_to(gvals[...].reshape(1, GW), gvs.shape)
    pl.semaphore_wait(barrier, 10)
    pending.append(chunk_send(d0))
    pending[-1].start()

    quarter = OUT_WIN // 4

    def gb_part(p, y_):
        rows = pl.ds(pl.multiple_of(p * GW, GW), GW)
        return g4.at[rows, pl.ds(pl.multiple_of(y_ * quarter, 128), quarter)]

    def gb_all(p):
        return g4.at[pl.ds(pl.multiple_of(p * GW, GW), GW)]

    p_partner = (1 - xh) * 2 + core
    chunk_own(d0, block0)

    def offset(direction, it):
        k = 4 - it
        return k if direction == 0 else (NZ - k) % NZ

    def ring_step(it, parity, own_half, sbuf, rbuf, ss, rs, sizes):
        for direction in range(2):
            half = parity if direction == 0 else 1 - parity
            size = sizes[half]
            d = (z + offset(direction, it)) % NZ
            srcs = list(own_half(d, half))
            rows = pl.ds(0, size)
            if it > parity:
                before = rbuf.at[direction, half, it - 1, rows]
                remote(
                    before, before, ss.at[direction, half, it - 1],
                    rs.at[direction, half, it - 1], ring[direction],
                ).wait_recv()
                srcs.append(load(rbuf.at[direction, half, it - 1]))
            add_rows(size, store(sbuf.at[direction, half, it]), srcs)
            send(
                sbuf.at[direction, half, it, rows], rbuf.at[direction, half, it, rows],
                ss.at[direction, half, it], rs.at[direction, half, it], ring[direction],
            )

    def ring_last(half, rbuf, ss, rs, sizes):
        rows = pl.ds(0, sizes[half])
        for direction in range(2):
            last = rbuf.at[direction, half, 3, rows]
            remote(
                last, last, ss.at[direction, half, 3], rs.at[direction, half, 3], ring[direction]
            ).wait_recv()
        return [load(rbuf.at[0, half, 3]), load(rbuf.at[1, half, 3])]

    a_sizes = (CH, CH)
    part_sizes = (CH // 2, CH // 2)
    gram_sizes = (GL, GR - GL)
    PART = CH // 2

    def chunks(ks):
        for k in ks:
            d, block = chunk(k)
            pending.append(chunk_send(d))
            pending[-1].start()
            chunk_own(d, block)

    def chunks_wait(ks):
        for k in ks:
            chunk_send((z + k) % NZ).wait_recv()

    def a_own(d, half):
        return load(own.at[d], half * CH), load(crecv.at[d], half * CH)

    def a_step(it, parity):
        ring_step(it, parity, a_own, asend, arecv, a_s, a_r, a_sizes)

    def bx_copy(d):
        return remote(xbs.at[d], xbr.at[d], xb_s.at[d], xb_r.at[d], partner)

    def bx_send(ks):
        for k in ks:
            d = (z + k) % NZ
            at = HALF + (1 - xh) * CH
            add_rows(CH, store(xbs.at[d]), [load(own.at[d], at), load(crecv.at[d], at)])
            copy = bx_copy(d)
            copy.start()
            pending.append(copy)

    def bx_wait(ks):
        for k in ks:
            bx_copy((z + k) % NZ).wait_recv()

    def b_own(d, half):
        at = HALF + xh * CH + half * PART
        return load(own.at[d], at), load(crecv.at[d], at), load(xbr.at[d], half * PART)

    def b_step(it, parity):
        ring_step(it, parity, b_own, bsend, brecv, b_s, b_r, part_sizes)

    def gram_g(first, last):
        mine = grads[:, pl.ds(pl.multiple_of(tensor * OB, 128), OB)]

        def body(i, _):
            at = pl.multiple_of(i * 384, 128)
            part = dot(grads[:, pl.ds(at, 384)], mine, TN)
            gramg[pl.ds(i * 4, 4)] = part.reshape(4, GW, OB)
            return 0

        lax.fori_loop(first, last, body, 0)

    def gram_a():
        def body(i, _):
            at = pl.multiple_of(i * 384, 128)
            part = dot(acts[:, pl.ds(at, 384)], acts[...], TN)
            grama[pl.ds(i * 16, 16)] = part.reshape(16, AW, 2 * CC)
            return 0

        lax.fori_loop(0, 2, body, 0)

    def gram_block(xh_, z_, core_):
        w = (xh_ * NZ + z_) * 2 + core_
        return gramg[inv[1, w, 0]], grama[inv[0, w, 0]]

    def put_block(ref, g_part, a_part):
        ref[0:GW, :] = g_part.astype(ref.dtype)
        tail = jnp.concatenate([a_part[:, 0:384], a_part[:, 384:768]], axis=0)
        ref[GW:GR, :] = tail.astype(ref.dtype)

    def gram_core(turn):
        other = 1 - xh if turn == 0 else xh

        def body(i, _):
            put_block(gcs.at[turn, i], *gram_block(other, i, 1 - core))
            return 0

        lax.fori_loop(0, NZ, body, 0)
        send(gcs.at[turn], gcr.at[turn], gc_s.at[turn], gc_r.at[turn], sibling)

    def gram_add(d, dst, xh_, others):
        put_block(gown.at[d], *gram_block(xh_, d, core))
        add_rows(GR, store(dst), [load(gown.at[d])] + [load(other) for other in others])

    def gx_copy(d):
        return remote(gxs.at[d], gxr.at[d], gx_s.at[d], gx_r.at[d], partner)

    def gram_wait(turn):
        remote(gcs.at[turn], gcr.at[turn], gc_s.at[turn], gc_r.at[turn], sibling).wait_recv()

    def gram_x(ks):
        for k in ks:
            d = (z + k) % NZ
            gram_add(d, gxs.at[d], 1 - xh, [gcr.at[0, d]])
            copy = gx_copy(d)
            copy.start()
            pending.append(copy)

    def gram_own(ks):
        for k in ks:
            d = (z + k) % NZ
            gx_copy(d).wait_recv()
            gram_add(d, gown.at[d], xh, [gcr.at[1, d], gxr.at[d]])

    def gram_half(d, half):
        return (load(gown.at[d], half * GL),)

    def gram_step(it, parity):
        ring_step(it, parity, gram_half, gsend, grecv, gz_s, gz_r, gram_sizes)

    def gather_copy(s, direction, half, it):
        b = (z + NZ - it) % NZ if direction == 0 else (z + it) % NZ
        part = eg.at[s, b, pl.ds(half * PART, PART)]
        return remote(
            part, part, e_s.at[s, direction, half, it], e_r.at[s, direction, half, it],
            ring[direction],
        )

    def gather(s, it):
        for half in (0, 1):
            for direction in (0, 1):
                side = half if direction == 0 else 1 - half
                if half == 1 and it == 3:
                    continue
                if it > 0:
                    gather_copy(s, direction, side, it - 1).wait_recv()
                copy = gather_copy(s, direction, side, it)
                copy.start()
                pending.append(copy)

    def gather_last(s):
        gather_copy(s, 0, 1, 2).wait_recv()
        gather_copy(s, 1, 0, 2).wait_recv()
        project(s, 3)
        project(s, 5)
        gather_copy(s, 0, 0, 3).wait_recv()
        gather_copy(s, 1, 1, 3).wait_recv()
        project(s, 4)

    def project(s, k):
        b = (z + k) % NZ
        part = dot(eg[s, b], g4[:, pl.ds(pl.multiple_of(b * OB, 128), OB)], NT)
        proj[s] = part if k == 0 else proj[s] + part

    def scale(s):
        g_row = jnp.concatenate([gv[p, 0:1, :] for p in range(4)], axis=1)
        first = core * CC + s * HALF + xh * CH

        def body(i, kl):
            at = pl.multiple_of(i * 16, 16)
            value = proj[s, pl.ds(at, 16), :]
            a_col = ab[pl.ds(pl.multiple_of(first + at, 16), 16), 0:1]
            scaled = value / (a_col * g_row + DAMPING)
            scl[s, pl.ds(at, 16), :] = scaled.astype(BF16)
            return kl + value * scaled

        return lax.fori_loop(0, CH // 16, body, jnp.zeros((16, OB), F32))

    def back_chunks(s, ks):
        for k in ks:
            d = (z + k) % NZ
            rown[s, d] = dot(scl[s], g4p[:, pl.ds(pl.multiple_of(d * OB, 128), OB)])

    def back_step(s, it, parity):
        def back_own(d, half):
            return (load(rown.at[s, d], half * PART),)

        ring_step(
            it, parity, back_own, rsend.at[s], rrecv.at[s], r_s.at[s], r_r.at[s], part_sizes
        )

    places = (
        (sibling, xh * 2 + 1 - core, (1 - core) * 2 + xh),
        (partner, (1 - xh) * 2 + core, core * 2 + 1 - xh),
        (partner_sibling, (1 - xh) * 2 + 1 - core, (1 - core) * 2 + 1 - xh),
    )
    j = core * 2 + xh

    def final_copy(s, n):
        to, p, _ = places[n]
        return remote(fsend.at[s, p], frecv.at[s, j], f_s.at[s, n], f_r.at[s, n], to)

    def final_keep(s):
        return pltpu.make_async_copy(fsend.at[s, me4], frecv.at[s, j], loc.at[4 + s])

    def final_send(s):
        for half in (0, 1):
            srcs = ring_last(half, rrecv.at[s], r_s.at[s], r_r.at[s], part_sizes)
            srcs.append(load(rown.at[s, z], half * PART))
            add_rows(PART, store(xown.at[pl.ds(half * PART, PART)]), srcs)
        turned = xown[...].T.astype(BF16)
        for p in range(4):
            fsend[s, p] = turned[p * GW : (p + 1) * GW, :]
        for n in (1, 2, 0):
            copy = final_copy(s, n)
            copy.start()
            pending.append(copy)
        final_keep(s).start()

    def final_dot(s):
        final_keep(s).wait()
        for n in (0, 1, 2):
            to, p, slot = places[n]
            remote(
                fsend.at[s, p], frecv.at[s, slot], f_s.at[s, n], f_r.at[s, n], to
            ).wait_recv()
        out = None
        for i in range(4):
            first = (i // 2) * CC + s * HALF + (i % 2) * CH
            part = dot(frecv[s, i], qat[first : first + CH, :])
            out = part if out is None else out + part
        return out

    def kl_round(stage, count, place, peer, buf, ss, rs):
        copies = []
        for k in range(1, count):
            send(klbuf.at[stage], buf.at[place(0)], ss.at[k], rs.at[place(0)], peer(k))
            copies.append(
                remote(klbuf.at[stage], buf.at[place(k)], ss.at[k], rs.at[place(k)], peer(k))
            )

        def finish():
            value = klbuf[stage]
            for k in range(1, count):
                copies[k - 1].wait_recv()
                value = value + buf[place(k)]
            klbuf[stage + 1] = value

        return finish

    def gb_forward():
        part = gb_part(p_partner, y)
        remote(part, part, gb_s.at[0], gb_r.at[y], partner).wait_recv()
        for k in range(1, 4):
            send(part, part, gb_s.at[k], gb_r.at[y], dev(y_=(y + k) % 4))
        send(gb_all(me4), gb_all(me4), gb_s.at[4], gb_r.at[4], sibling)

    def gb_sibling():
        for k in range(1, 4):
            y_ = (y + k) % 4
            there = gb_part(p_partner, y_)
            remote(there, there, gb_s.at[k], gb_r.at[y_], dev(y_=y_)).wait_recv()
        send(gb_all(p_partner), gb_all(p_partner), gb_s.at[5], gb_r.at[5], sibling)

    def gb_wait():
        for n, p in ((4, me4), (5, p_partner)):
            remote(gb_all(p), gb_all(p), gb_s.at[n], gb_r.at[n], sibling).wait_recv()

    others = (sibling, partner, partner_sibling)

    def gv_copy(n):
        return remote(gvs, gv.at[me4], gv_s.at[n], gv_r.at[n], others[n])

    def turn_columns():
        for i in range(NZ):
            for h in range(2):
                to = i * OB + h * HALF
                at = h * (OUT_WIN // 2) + i * HALF
                g4p[:, to : to + HALF] = g4[:, at : at + HALF]

    def a_last():
        for half in (0, 1):
            ring_last(half, arecv, a_s, a_r, a_sizes)

        def srcs(half):
            at = pl.multiple_of(half * CH, CH)
            return [
                load(own.at[z], at), load(crecv.at[z], at),
                load(arecv.at[0, half, 3]), load(arecv.at[1, half, 3]),
            ]

        add_rows(CH, store(xsend), srcs(1 - xh))
        send(xsend, xrecv, x_s.at[0], x_r.at[0], partner)
        add_rows(CH, store(xown), srcs(xh))

    def a_done():
        remote(xsend, xrecv, x_s.at[0], x_r.at[0], partner).wait_recv()
        add_rows(CH, store(eg.at[0, z]), [load(xown), load(xrecv)])

    def b_done():
        for half in (0, 1):
            srcs = ring_last(half, brecv, b_s, b_r, part_sizes) + list(b_own(z, half))
            add_rows(PART, store(eg.at[1, z, pl.ds(half * PART, PART)]), srcs)

    chunks((3, 5))
    chunks_wait((4,))
    a_step(0, 0)
    bx_send((4,))
    chunks_wait((3, 5))
    a_step(1, 1)
    bx_send((3, 5))
    send(gb_part(me4, y), gb_part(me4, y), gb_s.at[0], gb_r.at[y], partner)
    chunks((2, 6))
    gram_g(0, 2)
    a_step(1, 0)
    chunks_wait((2, 6))
    bx_send((2, 6))
    chunks((1, 7, 0))
    a_step(2, 1)
    bx_wait((4,))
    b_step(0, 0)
    chunks_wait((1, 7, 0))
    bx_send((1, 7, 0))
    gram_g(2, 3)
    a_step(2, 0)
    bx_wait((3, 5))
    b_step(1, 1)
    gram_g(3, 4)
    a_step(3, 1)
    b_step(1, 0)
    gram_g(4, 6)
    a_step(3, 0)
    gb_forward()
    for n in range(3):
        copy = gv_copy(n)
        copy.start()
        pending.append(copy)
    bx_wait((2, 6))
    b_step(2, 1)
    gram_g(6, 8)
    b_step(2, 0)
    gram_a()
    a_last()
    inv_copy.wait()
    gram_core(0)
    bx_wait((1, 7))
    b_step(3, 1)
    gram_core(1)
    b_step(3, 0)
    gram_wait(0)
    gram_x((4, 3, 5))
    a_done()
    gather(0, 0)
    bx_wait((0,))
    b_done()
    gather(1, 0)
    gram_x((2, 6, 1, 7, 0))
    gram_wait(1)
    gb_sibling()
    ab[...] = jnp.broadcast_to(avals[...].reshape(1, 2 * CC), (128, 2 * CC)).T
    gather(0, 1)
    gram_own((4,))
    gram_step(0, 0)
    gather(1, 1)
    gb_wait()
    project(0, 0)
    project(1, 0)
    gram_own((3, 5))
    gram_step(1, 1)
    for k in (1, 7):
        project(0, k)
    gather(0, 2)
    for k in (1, 7):
        project(1, k)
    gather(1, 2)
    gram_step(1, 0)
    turn_columns()
    for n in range(3):
        gv_copy(n).wait_recv()
    gv[me4] = gvs[...]
    for k in (2, 6):
        project(0, k)
    gather(0, 3)
    gram_own((2, 6))
    gram_step(2, 1)
    for k in (2, 6):
        project(1, k)
    gather(1, 3)
    gather_last(0)
    kl_a = scale(0)
    back_chunks(0, (4,))
    back_step(0, 0, 0)
    back_chunks(0, (3, 5))
    back_step(0, 1, 1)
    gather_last(1)
    kl_b = scale(1)
    klbuf[0] = jnp.full((8, 128), jnp.sum(kl_a + kl_b), F32)
    kl_z = kl_round(
        0, NZ, lambda k: (z + k) % NZ, lambda k: dev(z_=(z + k) % NZ), klz, klz_s, klz_r
    )
    back_chunks(1, (4,))
    back_step(1, 0, 0)
    back_chunks(1, (3, 5))
    back_step(1, 1, 1)
    back_chunks(0, (2, 6))
    back_step(0, 1, 0)
    back_step(0, 2, 1)
    back_chunks(1, (2, 6))
    back_step(1, 1, 0)
    back_step(1, 2, 1)
    gram_own((1, 7, 0))
    kl_z()
    kl_y = kl_round(
        1, 4, lambda k: (y + k) % 4, lambda k: dev(y_=(y + k) % 4), kly, kly_s, kly_r
    )
    back_chunks(0, (1, 7, 0))
    back_step(0, 2, 0)
    back_step(0, 3, 1)
    back_chunks(1, (1, 7, 0))
    back_step(1, 2, 0)
    back_step(1, 3, 1)
    gram_step(2, 0)
    kl_y()
    kl_x = kl_round(
        2, 4,
        lambda k: (xh ^ (k // 2)) * 2 + (xl ^ (k % 2)),
        lambda k: dev(xh_=xh ^ (k // 2), xl_=xl ^ (k % 2)),
        klx, klx_s, klx_r,
    )
    drain(24)
    back_step(0, 3, 0)
    back_step(1, 3, 0)
    gram_step(3, 1)
    gram_step(3, 0)
    kl_x()
    kl_c = kl_round(
        3, 2, lambda k: core if k == 0 else 1 - core, lambda k: sibling, klc, klc_s, klc_r
    )
    final_send(0)
    final_send(1)
    out_a = final_dot(0)
    total[...] = out_a
    kl_c()
    gain[...] = jnp.sqrt(OUT_WIN * FEAT / klbuf[4])
    drain(12)
    for half in (0, 1):
        srcs = ring_last(half, grecv, gz_s, gz_r, gram_sizes)
        srcs.append(load(gown.at[z], half * GL))
        size = gram_sizes[half]
        add_rows(size, store(gram.at[pl.ds(half * GL, size)]), srcs)
    total[...] = total[...] + final_dot(1)
    drain()


def finish(total, gram, gain, afac, gfac, update, new_a, new_g):
    update[...] = total[...] * gain[0:1, 0:1]
    fresh = (1.0 - DECAY) / TOKENS
    new_g[...] = DECAY * gfac[...] + fresh * gram[0:GW, :]
    new_a[:, 0:384] = DECAY * afac[:, 0:384] + fresh * gram[GW : GW + AW, :]
    new_a[:, 384:768] = DECAY * afac[:, 384:768] + fresh * gram[GW + AW : GR, :]


def per_device(
    activations, out_grads, a_basis, a_values, g_basis, g_values, owners, a_factors, g_factors
):
    vmem = pl.BlockSpec(memory_space=pltpu.VMEM)
    hbm = pl.BlockSpec(memory_space=pl.ANY)
    sem = pltpu.SemaphoreType.DMA
    v = pltpu.VMEM
    ring_a = (2, 2, 4, CH, OB)
    ring_b = (2, 2, 4, CH // 2, OB)
    scratch = [
        v((512, 768), BF16), v((512, OUT_WIN), BF16), v((768, 768), BF16),
        v((768, 768), BF16), v((768, 512), BF16), v((NZ, CC, OB), F32),
        v((NZ, CC, OB), BF16), v((NZ, CC, OB), BF16),
        v(ring_a, BF16), v(ring_a, BF16),
        v((CH, OB), BF16), v((CH, OB), BF16), v((CH, OB), F32),
        v((NZ, CH, OB), BF16), v((NZ, CH, OB), BF16), v(ring_b, BF16), v(ring_b, BF16),
        v((2, NZ, CH, OB), BF16), v((4 * GW, OUT_WIN), BF16), v((4 * GW, OUT_WIN), BF16),
        v((4, 8, GW), F32), v((8, GW), F32),
        v((768, 128), F32), v((2, CH, OB), F32), v((2, CH, OB), BF16),
        v((2, NZ, CH, OB), F32), v((2, *ring_b), BF16), v((2, *ring_b), BF16),
        v((2, 4, GW, CH), BF16), v((2, 4, GW, CH), BF16),
        v((32, GW, OB), F32), v((32, AW, 768), F32),
        v((2, NZ, GR, OB), BF16), v((2, NZ, GR, OB), BF16),
        v((NZ, GR, OB), BF16), v((NZ, GR, OB), BF16), v((NZ, GR, OB), F32),
        v((2, 2, 4, GL, OB), BF16), v((2, 2, 4, GL, OB), BF16),
        v((5, 8, 128), F32), v((NZ, 8, 128), F32), v((4, 8, 128), F32), v((4, 8, 128), F32),
        v((2, 8, 128), F32), v((2, 32, 128), jnp.int32), pltpu.SMEM((2, 32, 128), jnp.int32),
        sem((NZ,)), sem((NZ,)), sem((2, 2, 4)), sem((2, 2, 4)), sem((1,)), sem((1,)),
        sem((NZ,)), sem((NZ,)), sem((2, 2, 4)), sem((2, 2, 4)),
        sem((2, 2, 2, 4)), sem((2, 2, 2, 4)), sem((2, 2, 2, 4)), sem((2, 2, 2, 4)),
        sem((2, 3)), sem((2, 3)),
        sem((2,)), sem((2,)), sem((NZ,)), sem((NZ,)), sem((2, 2, 4)), sem((2, 2, 4)),
        sem((6,)), sem((6,)), sem((3,)), sem((3,)),
        sem((NZ,)), sem((NZ,)), sem((4,)), sem((4,)), sem((4,)), sem((4,)), sem((2,)), sem((2,)),
        sem((7,)),
    ]
    total, gram, gain = pl.pallas_call(
        kernel,
        out_shape=(
            jax.ShapeDtypeStruct((GW, 768), F32),
            jax.ShapeDtypeStruct((GR, OB), F32),
            jax.ShapeDtypeStruct((8, 128), F32),
        ),
        in_specs=[hbm] * 4 + [vmem] * 3,
        out_specs=(vmem, vmem, vmem),
        scratch_shapes=scratch,
        compiler_params=pltpu.CompilerParams(
            collective_id=0, has_side_effects=True, vmem_limit_bytes=60 << 20
        ),
        cost_estimate=pl.CostEstimate(
            flops=5_400_000_000, bytes_accessed=8_000_000, transcendentals=0
        ),
        name="precondition",
    )(activations, out_grads, a_basis, g_basis.T, a_values, g_values, owners)
    return pl.pallas_call(
        finish,
        out_shape=(
            jax.ShapeDtypeStruct((GW, 768), F32),
            jax.ShapeDtypeStruct((AW, 768), F32),
            jax.ShapeDtypeStruct((GW, OB), F32),
        ),
        in_specs=[vmem] * 5,
        out_specs=(vmem, vmem, vmem),
        name="finish",
    )(total, gram, gain, a_factors, g_factors)


def solution(mesh):
    in_specs = (
        P("dp", "tensor"),
        P("dp", None),
        P("tensor", None),
        P("tensor"),
        P(None, "dp"),
        P("dp"),
        P(),
        P("dp", "tensor"),
        P("dp", "tensor"),
    )
    out_specs = (P("dp", "tensor"), P("dp", "tensor"), P("dp", "tensor"))
    return jax.shard_map(
        per_device, mesh=mesh, in_specs=in_specs, out_specs=out_specs, check_vma=False
    )
```

```python
import functools

import jax
import jax.numpy as jnp
from jax import lax
from jax.experimental import pallas as pl
from jax.experimental.pallas import tpu as pltpu
from jax.sharding import PartitionSpec as P

FEAT = 6144
OUT_WIN = 3072
TOKENS = 16384
DECAY = 0.5
DAMPING = 0.1
F32 = jnp.float32
BF16 = jnp.bfloat16
MESH = pl.DeviceIdType.MESH

NZ = 8
CC = 384
HALF = 192
CH = 96
OB = 384
GW = 96
AW = 24
GR = 144
GL = 80

NT = (((1,), (1,)), ((), ()))
TN = (((0,), (0,)), ((), ()))


def dot(a, b, dims=(((1,), (0,)), ((), ()))):
    return lax.dot_general(a, b, dims, preferred_element_type=F32)


def add_rows(rows, dst, srcs):
    step = 48 if rows % 48 == 0 else 16

    def body(i, _):
        at = pl.ds(pl.multiple_of(i * step, step), step)
        total = srcs[0](at).astype(F32)
        for src in srcs[1:]:
            total = total + src(at).astype(F32)
        dst(at, total)
        return 0

    lax.fori_loop(0, rows // step, body, 0, unroll=rows // step)


def store(ref):
    def put(at, value):
        ref[at, :] = value.astype(ref.dtype)

    return put


def load(ref, first=0):
    def get(at):
        return ref[pl.ds(first + at.start, at.size), :]

    return get


def kernel(
    acts_in, grads_in, qa_in, gbasis_in, avals, gvals, owners,
    total, gram, gain,
    acts, grads, qa, qat, apt, own, csend, crecv,
    asend, arecv, xsend, xrecv, xown, xbs, xbr, bsend, brecv,
    eg, g4, g4p, gv, gvs, ab, den, proj, scl,
    rown, rsend, rrecv, fsend, frecv,
    gramg, grama, gcs, gcr, gxs, gxr, gown, gsend, grecv,
    klbuf, klz, kly, klx, klc, inv_rows, inv,
    c_s, c_r, a_s, a_r, x_s, x_r, xb_s, xb_r, b_s, b_r, e_s, e_r, r_s, r_r, f_s, f_r,
    gc_s, gc_r, gx_s, gx_r, gz_s, gz_r, gb_s, gb_r, gv_s, gv_r,
    klz_s, klz_r, kly_s, kly_r, klx_s, klx_r, klc_s, klc_r, loc,
):
    dp = lax.axis_index("dp")
    tensor = lax.axis_index("tensor")
    core = dp % 2
    z = (dp // 2) % NZ
    xh = dp // (2 * NZ)
    y = tensor // 2
    xl = tensor % 2

    def dev(xh_=xh, z_=z, core_=core, y_=y, xl_=xl):
        return ((xh_ * NZ + z_) * 2 + core_, y_ * 2 + xl_)

    sibling = dev(core_=1 - core)
    partner = dev(xh_=1 - xh)
    partner_sibling = dev(xh_=1 - xh, core_=1 - core)
    ring = (dev(z_=(z + 1) % NZ), dev(z_=(z + NZ - 1) % NZ))
    pending = []

    def remote(src, dst, ss, rs, to):
        return pltpu.make_async_remote_copy(
            src_ref=src, dst_ref=dst, send_sem=ss, recv_sem=rs, device_id=to, device_id_type=MESH
        )

    def send(*args):
        copy = remote(*args)
        copy.start()
        pending.append(copy)
        return copy

    def drain(keep=0):
        old = pending[: len(pending) - keep]
        for copy in old:
            copy.wait_send()
        del pending[: len(old)]

    barrier = pltpu.get_barrier_semaphore()

    def greet(to):
        pl.semaphore_signal(barrier, inc=1, device_id=to, device_id_type=MESH)

    me4 = xh * 2 + core
    mine4 = pl.ds(pl.multiple_of(me4 * GW, GW), GW)
    loads = [
        pltpu.make_async_copy(qa_in, qa, loc.at[0]),
        pltpu.make_async_copy(acts_in, acts, loc.at[1]),
        pltpu.make_async_copy(grads_in, grads, loc.at[2]),
        pltpu.make_async_copy(gbasis_in, g4.at[mine4], loc.at[3]),
    ]
    for copy in loads:
        copy.start()
    greet(sibling)
    greet(partner)
    greet(partner_sibling)
    greet(ring[0])
    greet(ring[1])
    for k in range(1, 4):
        greet(dev(y_=(y + k) % 4))
    greet(dev(xl_=1 - xl))
    greet(dev(xh_=1 - xh, xl_=1 - xl))

    for i in range(2):
        worker = lax.broadcasted_iota(jnp.int32, (32, 32), 0)
        block = lax.broadcasted_iota(jnp.int32, (32, 32), 1)
        here = jnp.where(jnp.broadcast_to(owners[i : i + 1, :], (32, 32)) == worker, block, 0)
        inv_rows[i] = jnp.broadcast_to(jnp.max(here, axis=1, keepdims=True), (32, 128))
    inv_copy = pltpu.make_async_copy(inv_rows, inv, loc.at[6])
    inv_copy.start()

    loads[0].wait()
    for i in range(6):
        qat[128 * i : 128 * (i + 1), :] = qa[:, 128 * i : 128 * (i + 1)].T
    loads[1].wait()
    for i in range(2):
        apt[384 * i : 384 * (i + 1), :] = dot(
            qat[384 * i : 384 * (i + 1), :], acts[...], NT
        ).astype(BF16)
    loads[2].wait()

    def chunk(k):
        d = (z + k) % NZ
        block = grads[:, pl.ds(pl.multiple_of(d * OB, 128), OB)]
        theirs = pl.ds(pl.multiple_of((1 - core) * CC, CC), CC)
        csend[d] = dot(apt[theirs, :], block).astype(BF16)
        return d, block

    def chunk_send(d):
        return remote(csend.at[d], crecv.at[d], c_s.at[d], c_r.at[d], sibling)

    def chunk_own(d, block):
        mine = pl.ds(pl.multiple_of(core * CC, CC), CC)
        own[d] = dot(apt[mine, :], block)

    d0, block0 = chunk(4)
    loads[3].wait()
    gvs[...] = jnp.broadcast_to(gvals[...].reshape(1, GW), gvs.shape)
    pl.semaphore_wait(barrier, 10)
    pending.append(chunk_send(d0))
    pending[-1].start()

    quarter = OUT_WIN // 4

    def gb_part(p, y_):
        rows = pl.ds(pl.multiple_of(p * GW, GW), GW)
        return g4.at[rows, pl.ds(pl.multiple_of(y_ * quarter, 128), quarter)]

    def gb_all(p):
        return g4.at[pl.ds(pl.multiple_of(p * GW, GW), GW)]

    p_partner = (1 - xh) * 2 + core
    chunk_own(d0, block0)

    def offset(direction, it):
        k = 4 - it
        return k if direction == 0 else (NZ - k) % NZ

    def ring_step(it, parity, own_half, sbuf, rbuf, ss, rs, sizes):
        for direction in range(2):
            half = parity if direction == 0 else 1 - parity
            size = sizes[half]
            d = (z + offset(direction, it)) % NZ
            srcs = list(own_half(d, half))
            rows = pl.ds(0, size)
            if it > parity:
                before = rbuf.at[direction, half, it - 1, rows]
                remote(
                    before, before, ss.at[direction, half, it - 1],
                    rs.at[direction, half, it - 1], ring[direction],
                ).wait_recv()
                srcs.append(load(rbuf.at[direction, half, it - 1]))
            add_rows(size, store(sbuf.at[direction, half, it]), srcs)
            send(
                sbuf.at[direction, half, it, rows], rbuf.at[direction, half, it, rows],
                ss.at[direction, half, it], rs.at[direction, half, it], ring[direction],
            )

    def ring_last(half, rbuf, ss, rs, sizes):
        rows = pl.ds(0, sizes[half])
        for direction in range(2):
            last = rbuf.at[direction, half, 3, rows]
            remote(
                last, last, ss.at[direction, half, 3], rs.at[direction, half, 3], ring[direction]
            ).wait_recv()
        return [load(rbuf.at[0, half, 3]), load(rbuf.at[1, half, 3])]

    a_sizes = (CH, CH)
    part_sizes = (CH // 2, CH // 2)
    gram_sizes = (GL, GR - GL)
    PART = CH // 2

    def chunks(ks):
        for k in ks:
            d, block = chunk(k)
            pending.append(chunk_send(d))
            pending[-1].start()
            chunk_own(d, block)

    def chunks_wait(ks):
        for k in ks:
            chunk_send((z + k) % NZ).wait_recv()

    def a_own(d, half):
        return load(own.at[d], half * CH), load(crecv.at[d], half * CH)

    def a_step(it, parity):
        ring_step(it, parity, a_own, asend, arecv, a_s, a_r, a_sizes)

    def bx_copy(d):
        return remote(xbs.at[d], xbr.at[d], xb_s.at[d], xb_r.at[d], partner)

    def bx_send(ks):
        for k in ks:
            d = (z + k) % NZ
            at = HALF + (1 - xh) * CH
            add_rows(CH, store(xbs.at[d]), [load(own.at[d], at), load(crecv.at[d], at)])
            copy = bx_copy(d)
            copy.start()
            pending.append(copy)

    def bx_wait(ks):
        for k in ks:
            bx_copy((z + k) % NZ).wait_recv()

    def b_own(d, half):
        at = HALF + xh * CH + half * PART
        return load(own.at[d], at), load(crecv.at[d], at), load(xbr.at[d], half * PART)

    def b_step(it, parity):
        ring_step(it, parity, b_own, bsend, brecv, b_s, b_r, part_sizes)

    def gram_g(first, last):
        mine = grads[:, pl.ds(pl.multiple_of(tensor * OB, 128), OB)]

        def body(i, _):
            at = pl.multiple_of(i * 384, 128)
            part = dot(grads[:, pl.ds(at, 384)], mine, TN)
            gramg[pl.ds(i * 4, 4)] = part.reshape(4, GW, OB)
            return 0

        lax.fori_loop(first, last, body, 0)

    def gram_a():
        def body(i, _):
            at = pl.multiple_of(i * 384, 128)
            part = dot(acts[:, pl.ds(at, 384)], acts[...], TN)
            grama[pl.ds(i * 16, 16)] = part.reshape(16, AW, 2 * CC)
            return 0

        lax.fori_loop(0, 2, body, 0)

    def gram_block(xh_, z_, core_):
        w = (xh_ * NZ + z_) * 2 + core_
        return gramg[inv[1, w, 0]], grama[inv[0, w, 0]]

    def put_block(ref, g_part, a_part):
        ref[0:GW, :] = g_part.astype(ref.dtype)
        tail = jnp.concatenate([a_part[:, 0:384], a_part[:, 384:768]], axis=0)
        ref[GW:GR, :] = tail.astype(ref.dtype)

    def gram_core(turn):
        other = 1 - xh if turn == 0 else xh

        def body(i, _):
            put_block(gcs.at[turn, i], *gram_block(other, i, 1 - core))
            return 0

        lax.fori_loop(0, NZ, body, 0)
        send(gcs.at[turn], gcr.at[turn], gc_s.at[turn], gc_r.at[turn], sibling)

    def gram_add(d, dst, xh_, others):
        put_block(gown.at[d], *gram_block(xh_, d, core))
        add_rows(GR, store(dst), [load(gown.at[d])] + [load(other) for other in others])

    def gx_copy(d):
        return remote(gxs.at[d], gxr.at[d], gx_s.at[d], gx_r.at[d], partner)

    def gram_wait(turn):
        remote(gcs.at[turn], gcr.at[turn], gc_s.at[turn], gc_r.at[turn], sibling).wait_recv()

    def gram_x(ks):
        for k in ks:
            d = (z + k) % NZ
            gram_add(d, gxs.at[d], 1 - xh, [gcr.at[0, d]])
            copy = gx_copy(d)
            copy.start()
            pending.append(copy)

    def gram_own(ks):
        for k in ks:
            d = (z + k) % NZ
            gx_copy(d).wait_recv()
            gram_add(d, gown.at[d], xh, [gcr.at[1, d], gxr.at[d]])

    def gram_half(d, half):
        return (load(gown.at[d], half * GL),)

    def gram_step(it, parity):
        ring_step(it, parity, gram_half, gsend, grecv, gz_s, gz_r, gram_sizes)

    def gather_copy(s, direction, half, it):
        b = (z + NZ - it) % NZ if direction == 0 else (z + it) % NZ
        part = eg.at[s, b, pl.ds(half * PART, PART)]
        return remote(
            part, part, e_s.at[s, direction, half, it], e_r.at[s, direction, half, it],
            ring[direction],
        )

    def gather(s, it):
        for half in (0, 1):
            for direction in (0, 1):
                side = half if direction == 0 else 1 - half
                if half == 1 and it == 3:
                    continue
                if it > 0:
                    gather_copy(s, direction, side, it - 1).wait_recv()
                copy = gather_copy(s, direction, side, it)
                copy.start()
                pending.append(copy)

    def gather_last(s):
        gather_copy(s, 0, 1, 2).wait_recv()
        gather_copy(s, 1, 0, 2).wait_recv()
        project(s, 3)
        project(s, 5)
        gather_copy(s, 0, 0, 3).wait_recv()
        gather_copy(s, 1, 1, 3).wait_recv()
        project(s, 4)

    def project(s, k):
        b = (z + k) % NZ
        part = dot(eg[s, b], g4[:, pl.ds(pl.multiple_of(b * OB, 128), OB)], NT)
        proj[s] = part if k == 0 else proj[s] + part

    def denominators(s):
        g_row = jnp.concatenate([gv[p, 0:1, :] for p in range(4)], axis=1)
        first = core * CC + s * HALF + xh * CH

        def body(i, _):
            at = pl.multiple_of(i * 16, 16)
            a_col = ab[pl.ds(pl.multiple_of(first + at, 16), 16), 0:1]
            den[s, pl.ds(at, 16), :] = a_col * g_row + DAMPING
            return 0

        lax.fori_loop(0, CH // 16, body, 0)

    def scale(s):
        def body(i, kl):
            at = pl.multiple_of(i * 16, 16)
            value = proj[s, pl.ds(at, 16), :]
            scaled = value / den[s, pl.ds(at, 16), :]
            scl[s, pl.ds(at, 16), :] = scaled.astype(BF16)
            return kl + value * scaled

        return lax.fori_loop(
            0, CH // 16, body, jnp.zeros((16, OB), F32), unroll=CH // 16
        )

    def back_chunks(s, ks):
        for k in ks:
            d = (z + k) % NZ
            rown[s, d] = dot(scl[s], g4p[:, pl.ds(pl.multiple_of(d * OB, 128), OB)])

    def back_step(s, it, parity):
        def back_own(d, half):
            return (load(rown.at[s, d], half * PART),)

        ring_step(
            it, parity, back_own, rsend.at[s], rrecv.at[s], r_s.at[s], r_r.at[s], part_sizes
        )

    places = (
        (sibling, xh * 2 + 1 - core, (1 - core) * 2 + xh),
        (partner, (1 - xh) * 2 + core, core * 2 + 1 - xh),
        (partner_sibling, (1 - xh) * 2 + 1 - core, (1 - core) * 2 + 1 - xh),
    )
    j = core * 2 + xh

    def final_copy(s, n):
        to, p, _ = places[n]
        return remote(fsend.at[s, p], frecv.at[s, j], f_s.at[s, n], f_r.at[s, n], to)

    def final_keep(s):
        return pltpu.make_async_copy(fsend.at[s, me4], frecv.at[s, j], loc.at[4 + s])

    def final_send(s):
        for half in (0, 1):
            srcs = ring_last(half, rrecv.at[s], r_s.at[s], r_r.at[s], part_sizes)
            srcs.append(load(rown.at[s, z], half * PART))
            add_rows(PART, store(xown.at[pl.ds(half * PART, PART)]), srcs)
        turned = xown[...].T.astype(BF16)
        for p in range(4):
            fsend[s, p] = turned[p * GW : (p + 1) * GW, :]
        for n in (1, 2, 0):
            copy = final_copy(s, n)
            copy.start()
            pending.append(copy)
        final_keep(s).start()

    def final_dot(s):
        final_keep(s).wait()
        for n in (0, 1, 2):
            to, p, slot = places[n]
            remote(
                fsend.at[s, p], frecv.at[s, slot], f_s.at[s, n], f_r.at[s, n], to
            ).wait_recv()
        out = None
        for i in range(4):
            first = (i // 2) * CC + s * HALF + (i % 2) * CH
            part = dot(frecv[s, i], qat[first : first + CH, :])
            out = part if out is None else out + part
        return out

    def kl_round(stage, count, place, peer, buf, ss, rs):
        copies = []
        for k in range(1, count):
            send(klbuf.at[stage], buf.at[place(0)], ss.at[k], rs.at[place(0)], peer(k))
            copies.append(
                remote(klbuf.at[stage], buf.at[place(k)], ss.at[k], rs.at[place(k)], peer(k))
            )

        def finish():
            value = klbuf[stage]
            for k in range(1, count):
                copies[k - 1].wait_recv()
                value = value + buf[place(k)]
            klbuf[stage + 1] = value

        return finish

    def gb_forward():
        part = gb_part(p_partner, y)
        remote(part, part, gb_s.at[0], gb_r.at[y], partner).wait_recv()
        for k in range(1, 4):
            send(part, part, gb_s.at[k], gb_r.at[y], dev(y_=(y + k) % 4))
        send(gb_all(me4), gb_all(me4), gb_s.at[4], gb_r.at[4], sibling)

    def gb_sibling():
        for k in range(1, 4):
            y_ = (y + k) % 4
            there = gb_part(p_partner, y_)
            remote(there, there, gb_s.at[k], gb_r.at[y_], dev(y_=y_)).wait_recv()
        send(gb_all(p_partner), gb_all(p_partner), gb_s.at[5], gb_r.at[5], sibling)

    def gb_wait():
        for n, p in ((4, me4), (5, p_partner)):
            remote(gb_all(p), gb_all(p), gb_s.at[n], gb_r.at[n], sibling).wait_recv()

    others = (sibling, partner, partner_sibling)

    def gv_copy(n):
        return remote(gvs, gv.at[me4], gv_s.at[n], gv_r.at[n], others[n])

    def turn_columns():
        for i in range(NZ):
            for h in range(2):
                to = i * OB + h * HALF
                at = h * (OUT_WIN // 2) + i * HALF
                g4p[:, to : to + HALF] = g4[:, at : at + HALF]

    def a_last():
        for half in (0, 1):
            ring_last(half, arecv, a_s, a_r, a_sizes)

        def srcs(half):
            at = pl.multiple_of(half * CH, CH)
            return [
                load(own.at[z], at), load(crecv.at[z], at),
                load(arecv.at[0, half, 3]), load(arecv.at[1, half, 3]),
            ]

        add_rows(CH, store(xsend), srcs(1 - xh))
        send(xsend, xrecv, x_s.at[0], x_r.at[0], partner)
        add_rows(CH, store(xown), srcs(xh))

    def a_done():
        remote(xsend, xrecv, x_s.at[0], x_r.at[0], partner).wait_recv()
        add_rows(CH, store(eg.at[0, z]), [load(xown), load(xrecv)])

    def b_done():
        for half in (0, 1):
            srcs = ring_last(half, brecv, b_s, b_r, part_sizes) + list(b_own(z, half))
            add_rows(PART, store(eg.at[1, z, pl.ds(half * PART, PART)]), srcs)

    chunks((3, 5))
    chunks_wait((4,))
    a_step(0, 0)
    bx_send((4,))
    chunks_wait((3, 5))
    a_step(1, 1)
    bx_send((3, 5))
    send(gb_part(me4, y), gb_part(me4, y), gb_s.at[0], gb_r.at[y], partner)
    chunks((2, 6))
    gram_g(0, 2)
    a_step(1, 0)
    chunks_wait((2, 6))
    bx_send((2, 6))
    chunks((1, 7, 0))
    a_step(2, 1)
    bx_wait((4,))
    b_step(0, 0)
    chunks_wait((1, 7, 0))
    bx_send((1, 7, 0))
    gram_g(2, 3)
    a_step(2, 0)
    bx_wait((3, 5))
    b_step(1, 1)
    gram_g(3, 4)
    a_step(3, 1)
    b_step(1, 0)
    gram_g(4, 6)
    a_step(3, 0)
    gb_forward()
    for n in range(3):
        copy = gv_copy(n)
        copy.start()
        pending.append(copy)
    bx_wait((2, 6))
    b_step(2, 1)
    gram_g(6, 8)
    b_step(2, 0)
    gram_a()
    a_last()
    inv_copy.wait()
    gram_core(0)
    bx_wait((1, 7))
    b_step(3, 1)
    gram_core(1)
    b_step(3, 0)
    gram_wait(0)
    gram_x((4, 3, 5))
    a_done()
    gather(0, 0)
    bx_wait((0,))
    b_done()
    gather(1, 0)
    gram_x((2, 6, 1, 7, 0))
    gram_wait(1)
    gb_sibling()
    ab[...] = jnp.broadcast_to(avals[...].reshape(1, 2 * CC), (128, 2 * CC)).T
    gather(0, 1)
    gram_own((4,))
    gram_step(0, 0)
    gather(1, 1)
    gb_wait()
    project(0, 0)
    project(1, 0)
    gram_own((3, 5))
    gram_step(1, 1)
    for k in (1, 7):
        project(0, k)
    gather(0, 2)
    for k in (1, 7):
        project(1, k)
    gather(1, 2)
    gram_step(1, 0)
    turn_columns()
    for n in range(3):
        gv_copy(n).wait_recv()
    gv[me4] = gvs[...]
    denominators(0)
    denominators(1)
    for k in (2, 6):
        project(0, k)
    gather(0, 3)
    gram_own((2, 6))
    gram_step(2, 1)
    for k in (2, 6):
        project(1, k)
    gather(1, 3)
    gather_last(0)
    kl_a = scale(0)
    back_chunks(0, (4,))
    back_step(0, 0, 0)
    back_chunks(0, (3, 5))
    back_step(0, 1, 1)
    gather_last(1)
    kl_b = scale(1)
    klbuf[0] = jnp.full((8, 128), jnp.sum(kl_a + kl_b), F32)
    kl_z = kl_round(
        0, NZ, lambda k: (z + k) % NZ, lambda k: dev(z_=(z + k) % NZ), klz, klz_s, klz_r
    )
    back_chunks(1, (4,))
    back_step(1, 0, 0)
    back_chunks(1, (3, 5))
    back_step(1, 1, 1)
    back_chunks(0, (2, 6))
    back_step(0, 1, 0)
    back_step(0, 2, 1)
    back_chunks(1, (2, 6))
    back_step(1, 1, 0)
    back_step(1, 2, 1)
    gram_own((1, 7, 0))
    kl_z()
    kl_y = kl_round(
        1, 4, lambda k: (y + k) % 4, lambda k: dev(y_=(y + k) % 4), kly, kly_s, kly_r
    )
    back_chunks(0, (1, 7, 0))
    back_step(0, 2, 0)
    back_step(0, 3, 1)
    back_chunks(1, (1, 7, 0))
    back_step(1, 2, 0)
    back_step(1, 3, 1)
    gram_step(2, 0)
    kl_y()
    kl_x = kl_round(
        2, 4,
        lambda k: (xh ^ (k // 2)) * 2 + (xl ^ (k % 2)),
        lambda k: dev(xh_=xh ^ (k // 2), xl_=xl ^ (k % 2)),
        klx, klx_s, klx_r,
    )
    drain(24)
    back_step(0, 3, 0)
    back_step(1, 3, 0)
    gram_step(3, 1)
    gram_step(3, 0)
    kl_x()
    kl_c = kl_round(
        3, 2, lambda k: core if k == 0 else 1 - core, lambda k: sibling, klc, klc_s, klc_r
    )
    final_send(0)
    final_send(1)
    out_a = final_dot(0)
    total[...] = out_a
    kl_c()
    gain[...] = jnp.sqrt(OUT_WIN * FEAT / klbuf[4])
    drain(12)
    for half in (0, 1):
        srcs = ring_last(half, grecv, gz_s, gz_r, gram_sizes)
        srcs.append(load(gown.at[z], half * GL))
        size = gram_sizes[half]
        add_rows(size, store(gram.at[pl.ds(half * GL, size)]), srcs)
    total[...] = total[...] + final_dot(1)
    drain()


def finish(total, gram, gain, afac, gfac, update, new_a, new_g):
    update[...] = total[...] * gain[0:1, 0:1]
    fresh = (1.0 - DECAY) / TOKENS
    new_g[...] = DECAY * gfac[...] + fresh * gram[0:GW, :]
    new_a[:, 0:384] = DECAY * afac[:, 0:384] + fresh * gram[GW : GW + AW, :]
    new_a[:, 384:768] = DECAY * afac[:, 384:768] + fresh * gram[GW + AW : GR, :]


def per_device(
    activations, out_grads, a_basis, a_values, g_basis, g_values, owners, a_factors, g_factors
):
    vmem = pl.BlockSpec(memory_space=pltpu.VMEM)
    hbm = pl.BlockSpec(memory_space=pl.ANY)
    sem = pltpu.SemaphoreType.DMA
    v = pltpu.VMEM
    ring_a = (2, 2, 4, CH, OB)
    ring_b = (2, 2, 4, CH // 2, OB)
    scratch = [
        v((512, 768), BF16), v((512, OUT_WIN), BF16), v((768, 768), BF16),
        v((768, 768), BF16), v((768, 512), BF16), v((NZ, CC, OB), F32),
        v((NZ, CC, OB), BF16), v((NZ, CC, OB), BF16),
        v(ring_a, BF16), v(ring_a, BF16),
        v((CH, OB), BF16), v((CH, OB), BF16), v((CH, OB), F32),
        v((NZ, CH, OB), BF16), v((NZ, CH, OB), BF16), v(ring_b, BF16), v(ring_b, BF16),
        v((2, NZ, CH, OB), BF16), v((4 * GW, OUT_WIN), BF16), v((4 * GW, OUT_WIN), BF16),
        v((4, 8, GW), F32), v((8, GW), F32),
        v((768, 128), F32), v((2, CH, OB), F32), v((2, CH, OB), F32), v((2, CH, OB), BF16),
        v((2, NZ, CH, OB), F32), v((2, *ring_b), BF16), v((2, *ring_b), BF16),
        v((2, 4, GW, CH), BF16), v((2, 4, GW, CH), BF16),
        v((32, GW, OB), F32), v((32, AW, 768), F32),
        v((2, NZ, GR, OB), BF16), v((2, NZ, GR, OB), BF16),
        v((NZ, GR, OB), BF16), v((NZ, GR, OB), BF16), v((NZ, GR, OB), F32),
        v((2, 2, 4, GL, OB), BF16), v((2, 2, 4, GL, OB), BF16),
        v((5, 8, 128), F32), v((NZ, 8, 128), F32), v((4, 8, 128), F32), v((4, 8, 128), F32),
        v((2, 8, 128), F32), v((2, 32, 128), jnp.int32), pltpu.SMEM((2, 32, 128), jnp.int32),
        sem((NZ,)), sem((NZ,)), sem((2, 2, 4)), sem((2, 2, 4)), sem((1,)), sem((1,)),
        sem((NZ,)), sem((NZ,)), sem((2, 2, 4)), sem((2, 2, 4)),
        sem((2, 2, 2, 4)), sem((2, 2, 2, 4)), sem((2, 2, 2, 4)), sem((2, 2, 2, 4)),
        sem((2, 3)), sem((2, 3)),
        sem((2,)), sem((2,)), sem((NZ,)), sem((NZ,)), sem((2, 2, 4)), sem((2, 2, 4)),
        sem((6,)), sem((6,)), sem((3,)), sem((3,)),
        sem((NZ,)), sem((NZ,)), sem((4,)), sem((4,)), sem((4,)), sem((4,)), sem((2,)), sem((2,)),
        sem((7,)),
    ]
    total, gram, gain = pl.pallas_call(
        kernel,
        out_shape=(
            jax.ShapeDtypeStruct((GW, 768), F32),
            jax.ShapeDtypeStruct((GR, OB), F32),
            jax.ShapeDtypeStruct((8, 128), F32),
        ),
        in_specs=[hbm] * 4 + [vmem] * 3,
        out_specs=(vmem, vmem, vmem),
        scratch_shapes=scratch,
        compiler_params=pltpu.CompilerParams(
            collective_id=0, has_side_effects=True, vmem_limit_bytes=60 << 20
        ),
        cost_estimate=pl.CostEstimate(
            flops=5_400_000_000, bytes_accessed=8_000_000, transcendentals=0
        ),
        name="precondition",
    )(activations, out_grads, a_basis, g_basis.T, a_values, g_values, owners)
    return pl.pallas_call(
        finish,
        out_shape=(
            jax.ShapeDtypeStruct((GW, 768), F32),
            jax.ShapeDtypeStruct((AW, 768), F32),
            jax.ShapeDtypeStruct((GW, OB), F32),
        ),
        in_specs=[vmem] * 5,
        out_specs=(vmem, vmem, vmem),
        name="finish",
    )(total, gram, gain, a_factors, g_factors)


def solution(mesh):
    in_specs = (
        P("dp", "tensor"),
        P("dp", None),
        P("tensor", None),
        P("tensor"),
        P(None, "dp"),
        P("dp"),
        P(),
        P("dp", "tensor"),
        P("dp", "tensor"),
    )
    out_specs = (P("dp", "tensor"), P("dp", "tensor"), P("dp", "tensor"))
    return jax.shard_map(
        per_device, mesh=mesh, in_specs=in_specs, out_specs=out_specs, check_vma=False
    )
```

```python
import functools

import jax
import jax.numpy as jnp
from jax import lax
from jax.experimental import pallas as pl
from jax.experimental.pallas import tpu as pltpu
from jax.sharding import PartitionSpec as P

FEAT = 6144
OUT_WIN = 3072
TOKENS = 16384
DECAY = 0.5
DAMPING = 0.1
F32 = jnp.float32
BF16 = jnp.bfloat16
MESH = pl.DeviceIdType.MESH

NZ = 8
CC = 384
HALF = 192
CH = 96
OB = 384
GW = 96
AW = 24
GR = 144
GL = 80

NT = (((1,), (1,)), ((), ()))
TN = (((0,), (0,)), ((), ()))


def dot(a, b, dims=(((1,), (0,)), ((), ()))):
    return lax.dot_general(a, b, dims, preferred_element_type=F32)


def add_rows(rows, dst, srcs):
    step = 48 if rows % 48 == 0 else 16

    def body(i, _):
        at = pl.ds(pl.multiple_of(i * step, step), step)
        total = srcs[0](at).astype(F32)
        for src in srcs[1:]:
            total = total + src(at).astype(F32)
        dst(at, total)
        return 0

    lax.fori_loop(0, rows // step, body, 0, unroll=rows // step)


def store(ref):
    def put(at, value):
        ref[at, :] = value.astype(ref.dtype)

    return put


def load(ref, first=0):
    def get(at):
        return ref[pl.ds(first + at.start, at.size), :]

    return get


def kernel(
    acts_in, grads_in, qa_in, gbasis_in, avals, gvals, owners,
    total, gram, gain,
    acts, grads, qa, qat, apt, own, csend, crecv,
    asend, arecv, xsend, xrecv, xown, xbs, xbr, bsend, brecv,
    eg, g4, g4p, gv, gvs, ab, den, proj, scl,
    rown, rsend, rrecv, fsend, frecv,
    gramg, grama, gcs, gcr, gxs, gxr, gown, gsend, grecv,
    klbuf, klz, kly, klx, klc, inv_rows, inv,
    c_s, c_r, a_s, a_r, x_s, x_r, xb_s, xb_r, b_s, b_r, e_s, e_r, r_s, r_r, f_s, f_r,
    gc_s, gc_r, gx_s, gx_r, gz_s, gz_r, gb_s, gb_r, gv_s, gv_r,
    klz_s, klz_r, kly_s, kly_r, klx_s, klx_r, klc_s, klc_r, loc,
):
    dp = lax.axis_index("dp")
    tensor = lax.axis_index("tensor")
    core = dp % 2
    z = (dp // 2) % NZ
    xh = dp // (2 * NZ)
    y = tensor // 2
    xl = tensor % 2

    def dev(xh_=xh, z_=z, core_=core, y_=y, xl_=xl):
        return ((xh_ * NZ + z_) * 2 + core_, y_ * 2 + xl_)

    sibling = dev(core_=1 - core)
    partner = dev(xh_=1 - xh)
    partner_sibling = dev(xh_=1 - xh, core_=1 - core)
    ring = (dev(z_=(z + 1) % NZ), dev(z_=(z + NZ - 1) % NZ))
    pending = []

    def remote(src, dst, ss, rs, to):
        return pltpu.make_async_remote_copy(
            src_ref=src, dst_ref=dst, send_sem=ss, recv_sem=rs, device_id=to, device_id_type=MESH
        )

    def send(*args):
        copy = remote(*args)
        copy.start()
        pending.append(copy)
        return copy

    def drain(keep=0):
        old = pending[: len(pending) - keep]
        for copy in old:
            copy.wait_send()
        del pending[: len(old)]

    barrier = pltpu.get_barrier_semaphore()

    def greet(to):
        pl.semaphore_signal(barrier, inc=1, device_id=to, device_id_type=MESH)

    me4 = xh * 2 + core
    mine4 = pl.ds(pl.multiple_of(me4 * GW, GW), GW)
    loads = [
        pltpu.make_async_copy(qa_in, qa, loc.at[0]),
        pltpu.make_async_copy(acts_in, acts, loc.at[1]),
        pltpu.make_async_copy(grads_in, grads, loc.at[2]),
        pltpu.make_async_copy(gbasis_in, g4.at[mine4], loc.at[3]),
    ]
    for copy in loads:
        copy.start()
    greet(sibling)
    greet(partner)
    greet(partner_sibling)
    greet(ring[0])
    greet(ring[1])
    for k in range(1, 4):
        greet(dev(y_=(y + k) % 4))
    greet(dev(xl_=1 - xl))
    greet(dev(xh_=1 - xh, xl_=1 - xl))

    for i in range(2):
        worker = lax.broadcasted_iota(jnp.int32, (32, 32), 0)
        block = lax.broadcasted_iota(jnp.int32, (32, 32), 1)
        here = jnp.where(jnp.broadcast_to(owners[i : i + 1, :], (32, 32)) == worker, block, 0)
        inv_rows[i] = jnp.broadcast_to(jnp.max(here, axis=1, keepdims=True), (32, 128))
    inv_copy = pltpu.make_async_copy(inv_rows, inv, loc.at[6])
    inv_copy.start()

    loads[0].wait()
    for i in range(6):
        qat[128 * i : 128 * (i + 1), :] = qa[:, 128 * i : 128 * (i + 1)].T
    loads[1].wait()
    for i in range(2):
        apt[384 * i : 384 * (i + 1), :] = dot(
            qat[384 * i : 384 * (i + 1), :], acts[...], NT
        ).astype(BF16)
    loads[2].wait()

    def chunk(k):
        d = (z + k) % NZ
        block = grads[:, pl.ds(pl.multiple_of(d * OB, 128), OB)]
        theirs = pl.ds(pl.multiple_of((1 - core) * CC, CC), CC)
        csend[d] = dot(apt[theirs, :], block).astype(BF16)
        return d, block

    def chunk_send(d):
        return remote(csend.at[d], crecv.at[d], c_s.at[d], c_r.at[d], sibling)

    def chunk_own(d, block):
        mine = pl.ds(pl.multiple_of(core * CC, CC), CC)
        own[d] = dot(apt[mine, :], block)

    d0, block0 = chunk(4)
    loads[3].wait()
    gvs[...] = jnp.broadcast_to(gvals[...].reshape(1, GW), gvs.shape)
    pl.semaphore_wait(barrier, 10)
    pending.append(chunk_send(d0))
    pending[-1].start()

    quarter = OUT_WIN // 4

    def gb_part(p, y_):
        rows = pl.ds(pl.multiple_of(p * GW, GW), GW)
        return g4.at[rows, pl.ds(pl.multiple_of(y_ * quarter, 128), quarter)]

    def gb_all(p):
        return g4.at[pl.ds(pl.multiple_of(p * GW, GW), GW)]

    p_partner = (1 - xh) * 2 + core
    chunk_own(d0, block0)

    def offset(direction, it):
        k = 4 - it
        return k if direction == 0 else (NZ - k) % NZ

    def ring_step(it, parity, own_half, sbuf, rbuf, ss, rs, sizes):
        for direction in range(2):
            half = parity if direction == 0 else 1 - parity
            size = sizes[half]
            d = (z + offset(direction, it)) % NZ
            srcs = list(own_half(d, half))
            rows = pl.ds(0, size)
            if it > parity:
                before = rbuf.at[direction, half, it - 1, rows]
                remote(
                    before, before, ss.at[direction, half, it - 1],
                    rs.at[direction, half, it - 1], ring[direction],
                ).wait_recv()
                srcs.append(load(rbuf.at[direction, half, it - 1]))
            add_rows(size, store(sbuf.at[direction, half, it]), srcs)
            send(
                sbuf.at[direction, half, it, rows], rbuf.at[direction, half, it, rows],
                ss.at[direction, half, it], rs.at[direction, half, it], ring[direction],
            )

    def ring_last(half, rbuf, ss, rs, sizes):
        rows = pl.ds(0, sizes[half])
        for direction in range(2):
            last = rbuf.at[direction, half, 3, rows]
            remote(
                last, last, ss.at[direction, half, 3], rs.at[direction, half, 3], ring[direction]
            ).wait_recv()
        return [load(rbuf.at[0, half, 3]), load(rbuf.at[1, half, 3])]

    a_sizes = (CH, CH)
    part_sizes = (CH // 2, CH // 2)
    gram_sizes = (GL, GR - GL)
    PART = CH // 2

    def chunks(ks):
        for k in ks:
            d, block = chunk(k)
            pending.append(chunk_send(d))
            pending[-1].start()
            chunk_own(d, block)

    def chunks_wait(ks):
        for k in ks:
            chunk_send((z + k) % NZ).wait_recv()

    def a_own(d, half):
        return load(own.at[d], half * CH), load(crecv.at[d], half * CH)

    def a_step(it, parity):
        ring_step(it, parity, a_own, asend, arecv, a_s, a_r, a_sizes)

    def bx_copy(d):
        return remote(xbs.at[d], xbr.at[d], xb_s.at[d], xb_r.at[d], partner)

    def bx_send(ks):
        for k in ks:
            d = (z + k) % NZ
            at = HALF + (1 - xh) * CH
            add_rows(CH, store(xbs.at[d]), [load(own.at[d], at), load(crecv.at[d], at)])
            copy = bx_copy(d)
            copy.start()
            pending.append(copy)

    def bx_wait(ks):
        for k in ks:
            bx_copy((z + k) % NZ).wait_recv()

    def b_own(d, half):
        at = HALF + xh * CH + half * PART
        return load(own.at[d], at), load(crecv.at[d], at), load(xbr.at[d], half * PART)

    def b_step(it, parity):
        ring_step(it, parity, b_own, bsend, brecv, b_s, b_r, part_sizes)

    def gram_g(first, last):
        mine = grads[:, pl.ds(pl.multiple_of(tensor * OB, 128), OB)]

        def body(i, _):
            at = pl.multiple_of(i * 384, 128)
            part = dot(grads[:, pl.ds(at, 384)], mine, TN)
            gramg[pl.ds(i * 4, 4)] = part.reshape(4, GW, OB)
            return 0

        lax.fori_loop(first, last, body, 0)

    def gram_a():
        def body(i, _):
            at = pl.multiple_of(i * 384, 128)
            part = dot(acts[:, pl.ds(at, 384)], acts[...], TN)
            grama[pl.ds(i * 16, 16)] = part.reshape(16, AW, 2 * CC)
            return 0

        lax.fori_loop(0, 2, body, 0)

    def gram_block(xh_, z_, core_):
        w = (xh_ * NZ + z_) * 2 + core_
        return gramg[inv[1, w, 0]], grama[inv[0, w, 0]]

    def put_block(ref, g_part, a_part):
        ref[0:GW, :] = g_part.astype(ref.dtype)
        tail = jnp.concatenate([a_part[:, 0:384], a_part[:, 384:768]], axis=0)
        ref[GW:GR, :] = tail.astype(ref.dtype)

    def gram_core(turn):
        other = 1 - xh if turn == 0 else xh

        def body(i, _):
            put_block(gcs.at[turn, i], *gram_block(other, i, 1 - core))
            return 0

        lax.fori_loop(0, NZ, body, 0)
        send(gcs.at[turn], gcr.at[turn], gc_s.at[turn], gc_r.at[turn], sibling)

    def gram_add(d, dst, xh_, others):
        put_block(gown.at[d], *gram_block(xh_, d, core))
        add_rows(GR, store(dst), [load(gown.at[d])] + [load(other) for other in others])

    def gx_copy(d):
        return remote(gxs.at[d], gxr.at[d], gx_s.at[d], gx_r.at[d], partner)

    def gram_wait(turn):
        remote(gcs.at[turn], gcr.at[turn], gc_s.at[turn], gc_r.at[turn], sibling).wait_recv()

    def gram_x(ks):
        for k in ks:
            d = (z + k) % NZ
            gram_add(d, gxs.at[d], 1 - xh, [gcr.at[0, d]])
            copy = gx_copy(d)
            copy.start()
            pending.append(copy)

    def gram_own(ks):
        for k in ks:
            d = (z + k) % NZ
            gx_copy(d).wait_recv()
            gram_add(d, gown.at[d], xh, [gcr.at[1, d], gxr.at[d]])

    def gram_half(d, half):
        return (load(gown.at[d], half * GL),)

    def gram_step(it, parity):
        ring_step(it, parity, gram_half, gsend, grecv, gz_s, gz_r, gram_sizes)

    def gather_copy(s, direction, half, it):
        b = (z + NZ - it) % NZ if direction == 0 else (z + it) % NZ
        part = eg.at[s, b, pl.ds(half * PART, PART)]
        return remote(
            part, part, e_s.at[s, direction, half, it], e_r.at[s, direction, half, it],
            ring[direction],
        )

    def gather(s, it):
        for half in (0, 1):
            for direction in (0, 1):
                side = half if direction == 0 else 1 - half
                if half == 1 and it == 3:
                    continue
                if it > 0:
                    gather_copy(s, direction, side, it - 1).wait_recv()
                copy = gather_copy(s, direction, side, it)
                copy.start()
                pending.append(copy)

    def gather_last(s):
        gather_copy(s, 0, 1, 2).wait_recv()
        gather_copy(s, 1, 0, 2).wait_recv()
        project(s, 3)
        project(s, 5)
        gather_copy(s, 0, 0, 3).wait_recv()
        gather_copy(s, 1, 1, 3).wait_recv()
        project(s, 4)

    def project(s, k):
        b = (z + k) % NZ
        part = dot(eg[s, b], g4[:, pl.ds(pl.multiple_of(b * OB, 128), OB)], NT)
        proj[s] = part if k == 0 else proj[s] + part

    def denominators(s):
        g_row = jnp.concatenate([gv[p, 0:1, :] for p in range(4)], axis=1)
        first = core * CC + s * HALF + xh * CH

        def body(i, _):
            at = pl.multiple_of(i * 16, 16)
            a_col = ab[pl.ds(pl.multiple_of(first + at, 16), 16), 0:1]
            den[s, pl.ds(at, 16), :] = a_col * g_row + DAMPING
            return 0

        lax.fori_loop(0, CH // 16, body, 0)

    def scale(s):
        def body(i, kl):
            at = pl.multiple_of(i * 16, 16)
            value = proj[s, pl.ds(at, 16), :]
            scaled = value / den[s, pl.ds(at, 16), :]
            scl[s, pl.ds(at, 16), :] = scaled.astype(BF16)
            return kl + value * scaled

        return lax.fori_loop(
            0, CH // 16, body, jnp.zeros((16, OB), F32), unroll=CH // 16
        )

    def back_chunks(s, ks):
        for k in ks:
            d = (z + k) % NZ
            rown[s, d] = dot(scl[s], g4p[:, pl.ds(pl.multiple_of(d * OB, 128), OB)])

    def back_step(s, it, parity):
        def back_own(d, half):
            return (load(rown.at[s, d], half * PART),)

        ring_step(
            it, parity, back_own, rsend.at[s], rrecv.at[s], r_s.at[s], r_r.at[s], part_sizes
        )

    places = (
        (sibling, xh * 2 + 1 - core, (1 - core) * 2 + xh),
        (partner, (1 - xh) * 2 + core, core * 2 + 1 - xh),
        (partner_sibling, (1 - xh) * 2 + 1 - core, (1 - core) * 2 + 1 - xh),
    )
    j = core * 2 + xh

    def final_copy(s, n):
        to, p, _ = places[n]
        return remote(fsend.at[s, p], frecv.at[s, j], f_s.at[s, n], f_r.at[s, n], to)

    def final_keep(s):
        return pltpu.make_async_copy(fsend.at[s, me4], frecv.at[s, j], loc.at[4 + s])

    def final_send(s):
        for half in (0, 1):
            srcs = ring_last(half, rrecv.at[s], r_s.at[s], r_r.at[s], part_sizes)
            srcs.append(load(rown.at[s, z], half * PART))
            add_rows(PART, store(xown.at[pl.ds(half * PART, PART)]), srcs)
        turned = xown[...].T.astype(BF16)
        for p in range(4):
            fsend[s, p] = turned[p * GW : (p + 1) * GW, :]
        for n in (1, 2, 0):
            copy = final_copy(s, n)
            copy.start()
            pending.append(copy)
        final_keep(s).start()

    def final_dot(s):
        final_keep(s).wait()
        for n in (0, 1, 2):
            to, p, slot = places[n]
            remote(
                fsend.at[s, p], frecv.at[s, slot], f_s.at[s, n], f_r.at[s, n], to
            ).wait_recv()
        out = None
        for i in range(4):
            first = (i // 2) * CC + s * HALF + (i % 2) * CH
            part = dot(frecv[s, i], qat[first : first + CH, :])
            out = part if out is None else out + part
        return out

    def kl_round(stage, count, place, peer, buf, ss, rs):
        copies = []
        for k in range(1, count):
            send(klbuf.at[stage], buf.at[place(0)], ss.at[k], rs.at[place(0)], peer(k))
            copies.append(
                remote(klbuf.at[stage], buf.at[place(k)], ss.at[k], rs.at[place(k)], peer(k))
            )

        def finish():
            value = klbuf[stage]
            for k in range(1, count):
                copies[k - 1].wait_recv()
                value = value + buf[place(k)]
            klbuf[stage + 1] = value

        return finish

    def gb_forward():
        part = gb_part(p_partner, y)
        remote(part, part, gb_s.at[0], gb_r.at[y], partner).wait_recv()
        for k in range(1, 4):
            send(part, part, gb_s.at[k], gb_r.at[y], dev(y_=(y + k) % 4))
        send(gb_all(me4), gb_all(me4), gb_s.at[4], gb_r.at[4], sibling)

    def gb_sibling():
        for k in range(1, 4):
            y_ = (y + k) % 4
            there = gb_part(p_partner, y_)
            remote(there, there, gb_s.at[k], gb_r.at[y_], dev(y_=y_)).wait_recv()
        send(gb_all(p_partner), gb_all(p_partner), gb_s.at[5], gb_r.at[5], sibling)

    def gb_wait():
        for n, p in ((4, me4), (5, p_partner)):
            remote(gb_all(p), gb_all(p), gb_s.at[n], gb_r.at[n], sibling).wait_recv()

    others = (sibling, partner, partner_sibling)

    def gv_copy(n):
        return remote(gvs, gv.at[me4], gv_s.at[n], gv_r.at[n], others[n])

    def turn_columns():
        for i in range(NZ):
            for h in range(2):
                to = i * OB + h * HALF
                at = h * (OUT_WIN // 2) + i * HALF
                g4p[:, to : to + HALF] = g4[:, at : at + HALF]

    def a_last():
        for half in (0, 1):
            ring_last(half, arecv, a_s, a_r, a_sizes)

        def srcs(half):
            at = pl.multiple_of(half * CH, CH)
            return [
                load(own.at[z], at), load(crecv.at[z], at),
                load(arecv.at[0, half, 3]), load(arecv.at[1, half, 3]),
            ]

        add_rows(CH, store(xsend), srcs(1 - xh))
        send(xsend, xrecv, x_s.at[0], x_r.at[0], partner)
        add_rows(CH, store(xown), srcs(xh))

    def a_done():
        remote(xsend, xrecv, x_s.at[0], x_r.at[0], partner).wait_recv()
        add_rows(CH, store(eg.at[0, z]), [load(xown), load(xrecv)])

    def b_done():
        for half in (0, 1):
            srcs = ring_last(half, brecv, b_s, b_r, part_sizes) + list(b_own(z, half))
            add_rows(PART, store(eg.at[1, z, pl.ds(half * PART, PART)]), srcs)

    chunks((3, 5))
    chunks_wait((4,))
    a_step(0, 0)
    bx_send((4,))
    chunks_wait((3, 5))
    a_step(1, 1)
    bx_send((3, 5))
    send(gb_part(me4, y), gb_part(me4, y), gb_s.at[0], gb_r.at[y], partner)
    chunks((2, 6))
    gram_g(0, 2)
    a_step(1, 0)
    chunks_wait((2, 6))
    bx_send((2, 6))
    chunks((1, 7, 0))
    a_step(2, 1)
    bx_wait((4,))
    b_step(0, 0)
    chunks_wait((1, 7, 0))
    bx_send((1, 7, 0))
    gram_g(2, 3)
    a_step(2, 0)
    bx_wait((3, 5))
    b_step(1, 1)
    gram_g(3, 4)
    a_step(3, 1)
    b_step(1, 0)
    gram_g(4, 6)
    a_step(3, 0)
    gb_forward()
    for n in range(3):
        copy = gv_copy(n)
        copy.start()
        pending.append(copy)
    bx_wait((2, 6))
    b_step(2, 1)
    gram_g(6, 8)
    b_step(2, 0)
    gram_a()
    a_last()
    inv_copy.wait()
    gram_core(0)
    bx_wait((1, 7))
    b_step(3, 1)
    gram_core(1)
    b_step(3, 0)
    gram_wait(0)
    gram_x((4, 3, 5))
    a_done()
    gather(0, 0)
    bx_wait((0,))
    b_done()
    gather(1, 0)
    gram_x((2, 6, 1, 7, 0))
    gram_wait(1)
    gb_sibling()
    ab[...] = jnp.broadcast_to(avals[...].reshape(1, 2 * CC), (128, 2 * CC)).T
    gather(0, 1)
    gram_own((4,))
    gram_step(0, 0)
    gather(1, 1)
    gb_wait()
    project(0, 0)
    project(1, 0)
    gram_own((3, 5))
    gram_step(1, 1)
    for k in (1, 7):
        project(0, k)
    gather(0, 2)
    for k in (1, 7):
        project(1, k)
    gather(1, 2)
    gram_step(1, 0)
    turn_columns()
    for n in range(3):
        gv_copy(n).wait_recv()
    gv[me4] = gvs[...]
    denominators(0)
    denominators(1)
    for k in (2, 6):
        project(0, k)
    gather(0, 3)
    gram_own((2, 6))
    gram_step(2, 1)
    for k in (2, 6):
        project(1, k)
    gather(1, 3)
    gather_last(0)
    kl_a = scale(0)
    back_chunks(0, (4,))
    back_step(0, 0, 0)
    back_chunks(0, (3, 5))
    back_step(0, 1, 1)
    gather_last(1)
    kl_b = scale(1)
    klbuf[0] = jnp.full((8, 128), jnp.sum(kl_a + kl_b), F32)
    kl_z = kl_round(
        0, NZ, lambda k: (z + k) % NZ, lambda k: dev(z_=(z + k) % NZ), klz, klz_s, klz_r
    )
    back_chunks(1, (4,))
    back_step(1, 0, 0)
    back_chunks(1, (3, 5))
    back_step(1, 1, 1)
    back_chunks(0, (2, 6))
    back_step(0, 1, 0)
    back_step(0, 2, 1)
    back_chunks(1, (2, 6))
    back_step(1, 1, 0)
    back_step(1, 2, 1)
    kl_z()
    kl_y = kl_round(
        1, 4, lambda k: (y + k) % 4, lambda k: dev(y_=(y + k) % 4), kly, kly_s, kly_r
    )
    gram_own((1, 7, 0))
    back_chunks(0, (1, 7, 0))
    back_step(0, 2, 0)
    back_step(0, 3, 1)
    back_chunks(1, (1, 7, 0))
    back_step(1, 2, 0)
    back_step(1, 3, 1)
    gram_step(2, 0)
    kl_y()
    kl_x = kl_round(
        2, 4,
        lambda k: (xh ^ (k // 2)) * 2 + (xl ^ (k % 2)),
        lambda k: dev(xh_=xh ^ (k // 2), xl_=xl ^ (k % 2)),
        klx, klx_s, klx_r,
    )
    drain(24)
    back_step(0, 3, 0)
    back_step(1, 3, 0)
    gram_step(3, 1)
    gram_step(3, 0)
    kl_x()
    kl_c = kl_round(
        3, 2, lambda k: core if k == 0 else 1 - core, lambda k: sibling, klc, klc_s, klc_r
    )
    final_send(0)
    final_send(1)
    out_a = final_dot(0)
    total[...] = out_a
    kl_c()
    gain[...] = jnp.sqrt(OUT_WIN * FEAT / klbuf[4])
    drain(12)
    for half in (0, 1):
        srcs = ring_last(half, grecv, gz_s, gz_r, gram_sizes)
        srcs.append(load(gown.at[z], half * GL))
        size = gram_sizes[half]
        add_rows(size, store(gram.at[pl.ds(half * GL, size)]), srcs)
    total[...] = total[...] + final_dot(1)
    drain()


def finish(total, gram, gain, afac, gfac, update, new_a, new_g):
    update[...] = total[...] * gain[0:1, 0:1]
    fresh = (1.0 - DECAY) / TOKENS
    new_g[...] = DECAY * gfac[...] + fresh * gram[0:GW, :]
    new_a[:, 0:384] = DECAY * afac[:, 0:384] + fresh * gram[GW : GW + AW, :]
    new_a[:, 384:768] = DECAY * afac[:, 384:768] + fresh * gram[GW + AW : GR, :]


def per_device(
    activations, out_grads, a_basis, a_values, g_basis, g_values, owners, a_factors, g_factors
):
    vmem = pl.BlockSpec(memory_space=pltpu.VMEM)
    hbm = pl.BlockSpec(memory_space=pl.ANY)
    sem = pltpu.SemaphoreType.DMA
    v = pltpu.VMEM
    ring_a = (2, 2, 4, CH, OB)
    ring_b = (2, 2, 4, CH // 2, OB)
    scratch = [
        v((512, 768), BF16), v((512, OUT_WIN), BF16), v((768, 768), BF16),
        v((768, 768), BF16), v((768, 512), BF16), v((NZ, CC, OB), F32),
        v((NZ, CC, OB), BF16), v((NZ, CC, OB), BF16),
        v(ring_a, BF16), v(ring_a, BF16),
        v((CH, OB), BF16), v((CH, OB), BF16), v((CH, OB), F32),
        v((NZ, CH, OB), BF16), v((NZ, CH, OB), BF16), v(ring_b, BF16), v(ring_b, BF16),
        v((2, NZ, CH, OB), BF16), v((4 * GW, OUT_WIN), BF16), v((4 * GW, OUT_WIN), BF16),
        v((4, 8, GW), F32), v((8, GW), F32),
        v((768, 128), F32), v((2, CH, OB), F32), v((2, CH, OB), F32), v((2, CH, OB), BF16),
        v((2, NZ, CH, OB), F32), v((2, *ring_b), BF16), v((2, *ring_b), BF16),
        v((2, 4, GW, CH), BF16), v((2, 4, GW, CH), BF16),
        v((32, GW, OB), F32), v((32, AW, 768), F32),
        v((2, NZ, GR, OB), BF16), v((2, NZ, GR, OB), BF16),
        v((NZ, GR, OB), BF16), v((NZ, GR, OB), BF16), v((NZ, GR, OB), F32),
        v((2, 2, 4, GL, OB), BF16), v((2, 2, 4, GL, OB), BF16),
        v((5, 8, 128), F32), v((NZ, 8, 128), F32), v((4, 8, 128), F32), v((4, 8, 128), F32),
        v((2, 8, 128), F32), v((2, 32, 128), jnp.int32), pltpu.SMEM((2, 32, 128), jnp.int32),
        sem((NZ,)), sem((NZ,)), sem((2, 2, 4)), sem((2, 2, 4)), sem((1,)), sem((1,)),
        sem((NZ,)), sem((NZ,)), sem((2, 2, 4)), sem((2, 2, 4)),
        sem((2, 2, 2, 4)), sem((2, 2, 2, 4)), sem((2, 2, 2, 4)), sem((2, 2, 2, 4)),
        sem((2, 3)), sem((2, 3)),
        sem((2,)), sem((2,)), sem((NZ,)), sem((NZ,)), sem((2, 2, 4)), sem((2, 2, 4)),
        sem((6,)), sem((6,)), sem((3,)), sem((3,)),
        sem((NZ,)), sem((NZ,)), sem((4,)), sem((4,)), sem((4,)), sem((4,)), sem((2,)), sem((2,)),
        sem((7,)),
    ]
    total, gram, gain = pl.pallas_call(
        kernel,
        out_shape=(
            jax.ShapeDtypeStruct((GW, 768), F32),
            jax.ShapeDtypeStruct((GR, OB), F32),
            jax.ShapeDtypeStruct((8, 128), F32),
        ),
        in_specs=[hbm] * 4 + [vmem] * 3,
        out_specs=(vmem, vmem, vmem),
        scratch_shapes=scratch,
        compiler_params=pltpu.CompilerParams(
            collective_id=0, has_side_effects=True, vmem_limit_bytes=60 << 20
        ),
        cost_estimate=pl.CostEstimate(
            flops=5_400_000_000, bytes_accessed=8_000_000, transcendentals=0
        ),
        name="precondition",
    )(activations, out_grads, a_basis, g_basis.T, a_values, g_values, owners)
    return pl.pallas_call(
        finish,
        out_shape=(
            jax.ShapeDtypeStruct((GW, 768), F32),
            jax.ShapeDtypeStruct((AW, 768), F32),
            jax.ShapeDtypeStruct((GW, OB), F32),
        ),
        in_specs=[vmem] * 5,
        out_specs=(vmem, vmem, vmem),
        name="finish",
    )(total, gram, gain, a_factors, g_factors)


def solution(mesh):
    in_specs = (
        P("dp", "tensor"),
        P("dp", None),
        P("tensor", None),
        P("tensor"),
        P(None, "dp"),
        P("dp"),
        P(),
        P("dp", "tensor"),
        P("dp", "tensor"),
    )
    out_specs = (P("dp", "tensor"), P("dp", "tensor"), P("dp", "tensor"))
    return jax.shard_map(
        per_device, mesh=mesh, in_specs=in_specs, out_specs=out_specs, check_vma=False
    )
```
